32 devices in a mesh: clip: 4 (over y, core), seq: 8 (over z, x).
Axes of the slice: x: 2, y: 2, z: 4, core: 2. Of those that a mesh axis runs over, the one named last changes fastest.
Arguments:
- tokens: bfloat16 [4, 1024, 1536], P('clip', 'seq'), may hold values from -6 to 6
- caption: bfloat16 [4, 256, 4096], P('clip', 'seq'), may hold values from -6 to 6
- lengths: int32 [4], P('clip'), may hold values from 128 to 256, as said below
- timesteps: int32 [4], P('clip'), may hold values from 0 to 999
- positions: int32 [3, 4, 1024], P(None, 'clip', 'seq'), may hold values from 0 to 63
- w_time: bfloat16 [256, 1024], P(('clip', 'seq')), may hold values from -0.375 to 0.375
- w_pool: bfloat16 [4096, 1024], P(('clip', 'seq')), may hold values from -0.09375 to 0.09375
- w_ada: bfloat16 [1024, 6144], P(('clip', 'seq')), may hold values from -0.09375 to 0.09375
- b_ada: float32 [6144], replicated, may hold values from -2 to 2
- norm1_gain: float32 [1536], replicated, may hold values from 0.25 to 1.75
- w_qkv: bfloat16 [1536, 4608], P(('clip', 'seq')), may hold values from -0.15625 to 0.15625
- w_key_text: bfloat16 [4096, 1536], P(('clip', 'seq')), may hold values from -0.09375 to 0.09375
- w_value_text: bfloat16 [4096, 1536], P(('clip', 'seq')), may hold values from -0.09375 to 0.09375
- cross_gate: float32 [24], replicated, may hold values from 0.2 to 0.8
- w_out: bfloat16 [1536, 1536], P(('clip', 'seq')), may hold values from -1.25 to 1.25
- norm2_gain: float32 [1536], replicated, may hold values from 0.25 to 1.75
- w_gate: bfloat16 [1536, 4096], P(('clip', 'seq')), may hold values from -0.15625 to 0.15625
- w_up: bfloat16 [1536, 4096], P(('clip', 'seq')), may hold values from -0.15625 to 0.15625
- w_down: bfloat16 [4096, 1536], P(('clip', 'seq')), may hold values from -0.09375 to 0.09375
- cotangent: bfloat16 [4, 1024, 1536], P('clip', 'seq'), may hold values from -6 to 6
Outputs:
- mixed_out: bfloat16 [4, 1024, 1536], P('clip', 'seq')
- grad_tokens: float32 [4, 1024, 1536], P('clip', 'seq')
- grad_caption: float32 [4, 256, 4096], P('clip', 'seq')
- grad_w_time: float32 [256, 1024], P(('clip', 'seq'))
- grad_w_pool: float32 [4096, 1024], P(('clip', 'seq'))
- grad_w_ada: float32 [1024, 6144], P(('clip', 'seq'))
- grad_b_ada: float32 [6144], replicated
- grad_norm1_gain: float32 [1536], replicated
- grad_w_qkv: float32 [1536, 4608], P(('clip', 'seq'))
- grad_w_key_text: float32 [4096, 1536], P(('clip', 'seq'))
- grad_w_value_text: float32 [4096, 1536], P(('clip', 'seq'))
- grad_cross_gate: float32 [24], replicated
- grad_w_out: float32 [1536, 1536], P(('clip', 'seq'))
- grad_norm2_gain: float32 [1536], replicated
- grad_w_gate: float32 [1536, 4096], P(('clip', 'seq'))
- grad_w_up: float32 [1536, 4096], P(('clip', 'seq'))
- grad_w_down: float32 [4096, 1536], P(('clip', 'seq'))
The draws below stay inside these ranges and needn't reach their ends.
Inputs may be any that keep to these rules, and one draw needn't show every extreme that they name: caption slots below lengths[c] hold the caption of clip c; in every draw some clip has all 256 slots.
All inputs are finite; a program needn't handle non-finite values.
Results may differ from the reference program's by a relative error of at most 0.018.
Values may be sent and summed in bfloat16 or wider, within the bound.
No kernel may reach another device: no remote copies, remote signals or barrier semaphores. Data moves between devices by JAX's collectives and lax.ppermute only.
A program may use at most 448 MiB of HBM per device.

```python
import math
import jax
import jax.numpy as jnp
from jax import lax

D = 1536
HEADS = 24
HD = 64
FF = 4096
DT = 4096
CD = 1024
TE = 256
CAP = 256
CLIPS = 4
SEQLEN = 1024


def draw_lengths(key, part):
    key = jax.random.fold_in(key, 7)
    length_key, chosen_key = jax.random.split(key)
    drawn_lengths = jax.random.randint(length_key, (CLIPS,), CAP // 2, CAP + 1)
    chosen = jax.random.randint(chosen_key, (), 0, CLIPS)
    return jnp.where(jnp.arange(CLIPS) == chosen, CAP, drawn_lengths).astype(jnp.int32)


def plant(result, stream_key, low, largest):
    shape = result.shape
    spot = [jax.random.randint(jax.random.fold_in(stream_key, axis), (), 0, shape[axis]) for axis in range(len(shape))]
    result = result.at[tuple(spot)].set(low)
    longest = shape.index(max(shape))
    spot[longest] = (spot[longest] + 1) % shape[longest]
    return result.at[tuple(spot)].set(largest)


def level_of(stream_key, extent, cuts, least, top_value):
    level, own = 1.0, jax.random.fold_in(stream_key, 6)
    for position, shards_of in cuts:
        heights = jnp.exp(jax.random.uniform(jax.random.fold_in(own, position), (shards_of,), jnp.float32, least / len(cuts), top_value / len(cuts)))
        level = level * jnp.repeat(heights, extent[position] // shards_of).reshape([-1 if axis == position else 1 for axis in range(len(extent))])
    return level


def bell_draw(stream_key, extent, width, bound, cuts=(), kind=jnp.bfloat16):
    drawn = jax.random.normal(stream_key, extent, jnp.float32) * width
    if len(cuts) > 0:
        drawn = level_of(stream_key, extent, cuts, -0.22, 0.18) * drawn
    return jnp.clip(drawn, min=-bound, max=bound).astype(kind)


def setup_inputs(seed: int = 0) -> dict:
    seeds = jax.random.split(jax.random.key(seed), 21)
    tokens = bell_draw(seeds[0], (CLIPS, SEQLEN, D), 1.0, 6.0, ((0, 4), (1, 8)))
    caption = bell_draw(seeds[1], (CLIPS, CAP, DT), 1.0, 6.0, ((0, 4), (1, 8)))
    lengths = draw_lengths(jax.random.fold_in(seeds[20], 71), 0)
    timesteps = plant(jax.random.randint(seeds[3], (CLIPS,), 0, 1000), jax.random.fold_in(seeds[3], 1), 0, 999).astype(jnp.int32)
    positions = plant(jax.random.randint(seeds[4], (3, CLIPS, SEQLEN), 0, 64), jax.random.fold_in(seeds[4], 1), 0, 63).astype(jnp.int32)
    w_time = bell_draw(seeds[5], (TE, CD), TE ** -0.5, 0.375, ((0, 32),))
    w_pool = bell_draw(seeds[6], (DT, CD), DT ** -0.5, 0.09375, ((0, 32),))
    w_ada = bell_draw(seeds[7], (CD, 4 * D), (4 * CD) ** -0.5, 0.09375, ((0, 32),))
    b_ada = bell_draw(seeds[8], (4 * D,), 0.3, 2.0, (), jnp.float32)
    norm1_gain = jnp.clip(1.0 + 0.15 * jax.random.normal(seeds[9], (D,), jnp.float32), 0.25, 1.75)
    w_qkv = bell_draw(seeds[10], (D, 3 * D), D ** -0.5, 0.15625, ((0, 32),))
    w_key_text = bell_draw(seeds[11], (DT, D), DT ** -0.5, 0.09375, ((0, 32),))
    w_value_text = bell_draw(seeds[12], (DT, D), DT ** -0.5, 0.09375, ((0, 32),))
    cross_gate = jnp.clip(jax.random.uniform(seeds[13], (HEADS,), jnp.float32, 0.2, 0.8), 0.2, 0.8)
    w_out = bell_draw(seeds[14], (D, D), (max(1, D // 64)) ** -0.5, 1.25, ((0, 32),))
    norm2_gain = jnp.clip(1.0 + 0.15 * jax.random.normal(seeds[15], (D,), jnp.float32), 0.25, 1.75)
    w_gate = bell_draw(seeds[16], (D, FF), D ** -0.5, 0.15625, ((0, 32),))
    w_up = bell_draw(seeds[17], (D, FF), D ** -0.5, 0.15625, ((0, 32),))
    w_down = bell_draw(seeds[18], (FF, D), FF ** -0.5, 0.09375, ((0, 32),))
    cotangent = bell_draw(seeds[19], (CLIPS, SEQLEN, D), 1.0, 6.0, ((0, 4), (1, 8)))
    return dict(tokens=tokens, caption=caption, lengths=lengths, timesteps=timesteps, positions=positions, w_time=w_time, w_pool=w_pool, w_ada=w_ada, b_ada=b_ada, norm1_gain=norm1_gain, w_qkv=w_qkv, w_key_text=w_key_text, w_value_text=w_value_text, cross_gate=cross_gate, w_out=w_out, norm2_gain=norm2_gain, w_gate=w_gate, w_up=w_up, w_down=w_down, cotangent=cotangent)


epsilon = 1e-05
head_eps = 1e-06
highest = lax.Precision.HIGHEST

@jax.custom_vjp
def low(v):
    return lax.optimization_barrier(v.astype(jnp.bfloat16)).astype(jnp.float32)

@jax.custom_vjp
def low_back(v):
    return v

def low_keep(v):
    return (low(v), None)

def low_pass(kept, grad):
    return (grad,)

def back_keep(v):
    return (v, None)

def back_low(kept, grad):
    return (low(grad),)
low.defvjp(low_keep, low_pass)
low_back.defvjp(back_keep, back_low)

def rope_tables(posint, half_dim):
    pair_ids = jnp.arange(half_dim)
    first_cut = half_dim // 4
    second_cut = first_cut + (half_dim - first_cut) // 2
    group_of = (pair_ids >= first_cut).astype(jnp.int32) + (pair_ids >= second_cut).astype(jnp.int32)
    starts = jnp.where(group_of == 0, 0, jnp.where(group_of == 1, first_cut, second_cut))
    counts = jnp.where(group_of == 0, first_cut, jnp.where(group_of == 1, second_cut - first_cut, half_dim - second_cut))
    frequency = jnp.exp(-math.log(10000.0) * (pair_ids - starts).astype(jnp.float32) / counts.astype(jnp.float32))
    onehot = (group_of[:, None] == jnp.arange(3)[None, :]).astype(jnp.float32)
    coords = jnp.dot(onehot, posint.astype(jnp.float32), precision=highest)
    angles = coords.T * frequency[None, :]
    return (jnp.cos(angles), jnp.sin(angles))

def rotate(vector, cos_tab, sin_tab):
    half_dim = cos_tab.shape[-1]
    front = vector[..., :half_dim]
    behind = vector[..., half_dim:]
    cos_b = cos_tab[:, None, :]
    sin_b = sin_tab[:, None, :]
    return jnp.concatenate([front * cos_b - behind * sin_b, front * sin_b + behind * cos_b], -1)

def head_norm(vector):
    return vector * lax.rsqrt(lax.optimization_barrier(jnp.mean(vector * vector, -1, keepdims=True)) + head_eps)

def timestep_embed(time_step, embed_width):
    half_dim = embed_width // 2
    frequency = jnp.exp(-math.log(10000.0) * jnp.arange(half_dim, dtype=jnp.float32) / half_dim)
    angles = time_step.astype(jnp.float32) * frequency
    return jnp.concatenate([jnp.cos(angles), jnp.sin(angles)])

def self_block(query_block, keys_b, values_b):
    scores = low_back(jnp.einsum('qhd,khd->hqk', query_block, keys_b, precision=highest) * (1.0 / math.sqrt(HD)))
    soft_probs = jax.nn.softmax(scores, axis=-1)
    return jnp.einsum('hqk,khd->qhd', low(soft_probs), values_b, precision=highest)

def block_forward(tokens_f, caption_f, length, time_step, posint, w_time, w_pool, w_ada, b_ada, norm1_gain, w_qkv, w_key_text, w_value_text, cross_gate, w_out, norm2_gain, w_gate, w_up, w_down):
    attn_scale = 1.0 / math.sqrt(HD)
    cap_mask = (jnp.arange(CAP) < length).astype(jnp.float32)
    length_f = length.astype(jnp.float32)
    pooled = lax.optimization_barrier(jnp.sum(caption_f * cap_mask[:, None], 0)) / length_f
    time_embed = timestep_embed(time_step, TE)
    condition = jnp.dot(low(time_embed)[None], w_time, precision=highest) + jnp.dot(low(pooled)[None], w_pool, precision=highest)
    modulation = jnp.dot(low(jax.nn.silu(condition)), w_ada, precision=highest) + b_ada[None]
    scale_attn, gate_attn, scale_ffn, gate_ffn = jnp.split(modulation[0], 4)
    normed1 = tokens_f * lax.rsqrt(lax.optimization_barrier(jnp.mean(tokens_f * tokens_f, -1, keepdims=True)) + epsilon)
    mix_in = low(normed1 * norm1_gain * (1.0 + scale_attn))
    qkv_all = low_back(jnp.dot(mix_in, w_qkv, precision=highest))
    queries = qkv_all[:, :D].reshape(SEQLEN, HEADS, HD)
    keys_raw = qkv_all[:, D:2 * D].reshape(SEQLEN, HEADS, HD)
    values = qkv_all[:, 2 * D:].reshape(SEQLEN, HEADS, HD)
    cos_tab, sin_tab = rope_tables(posint, HD // 2)
    queries_b = low(rotate(head_norm(queries), cos_tab, sin_tab))
    keys_b = low(rotate(head_norm(keys_raw), cos_tab, sin_tab))
    values_b = low(values)
    query_rows = min(512, SEQLEN)
    blocks = queries_b.reshape(SEQLEN // query_rows, query_rows, HEADS, HD)
    self_out = lax.map(jax.checkpoint(lambda query_block: self_block(query_block, keys_b, values_b)), blocks)
    self_out = low_back(self_out.reshape(SEQLEN, HEADS, HD))
    text_keys = head_norm(low_back(jnp.dot(low(caption_f), w_key_text, precision=highest)).reshape(CAP, HEADS, HD))
    text_values = low_back(jnp.dot(low(caption_f), w_value_text, precision=highest)).reshape(CAP, HEADS, HD)
    keys_text_b = low(text_keys)
    values_text_b = low(text_values)
    cross_scores = low_back(jnp.einsum('qhd,khd->hqk', queries_b, keys_text_b, precision=highest) * attn_scale)
    cross_scores = jnp.where(cap_mask[None, None, :] > 0, cross_scores, -1e+30)
    cross_probs = jax.nn.softmax(cross_scores, axis=-1)
    cross_out = low_back(jnp.einsum('hqk,khd->qhd', low(cross_probs), values_text_b, precision=highest))
    mixed = self_out + jnp.tanh(cross_gate)[None, :, None] * cross_out
    mixed_b = low(mixed.reshape(SEQLEN, D))
    attn_out = low_back(jnp.dot(mixed_b, w_out, precision=highest))
    resid = tokens_f + jnp.tanh(gate_attn) * attn_out
    normed2 = resid * lax.rsqrt(lax.optimization_barrier(jnp.mean(resid * resid, -1, keepdims=True)) + epsilon)
    ffn_in = low(normed2 * norm2_gain * (1.0 + scale_ffn))
    gate_pre = low_back(jnp.dot(ffn_in, w_gate, precision=highest))
    up_pre = low_back(jnp.dot(ffn_in, w_up, precision=highest))
    hidden_b = low(jax.nn.silu(gate_pre) * up_pre)
    ffn_out = low_back(jnp.dot(hidden_b, w_down, precision=highest))
    return resid + jnp.tanh(gate_ffn) * ffn_out

def reference(tokens, caption, lengths, timesteps, positions, w_time, w_pool, w_ada, b_ada, norm1_gain, w_qkv, w_key_text, w_value_text, cross_gate, w_out, norm2_gain, w_gate, w_up, w_down, cotangent):
    weights = tuple((weight.astype(jnp.float32) for weight in (w_time, w_pool, w_ada, b_ada, norm1_gain, w_qkv, w_key_text, w_value_text, cross_gate, w_out, norm2_gain, w_gate, w_up, w_down)))

    def forward(tokens_f, caption_f, *params):
        outputs = [block_forward(tokens_f[clip_index], caption_f[clip_index], lengths[clip_index], timesteps[clip_index], positions[:, clip_index, :], *params) for clip_index in range(CLIPS)]
        return jnp.stack(outputs)
    primal, pullback = jax.vjp(forward, tokens.astype(jnp.float32), caption.astype(jnp.float32), *weights)
    grads = pullback(cotangent.astype(jnp.float32))
    return (primal.astype(jnp.bfloat16), grads[0], grads[1], grads[2], grads[3], grads[4], grads[5], grads[6], grads[7], grads[8], grads[9], grads[10], grads[11], grads[12], grads[13], grads[14], grads[15])
```

```python
import math

import jax
import jax.numpy as jnp
from jax import lax
from jax.sharding import Mesh
from jax.sharding import PartitionSpec as P

epsilon = 1e-05
head_eps = 1e-06
big_negative = -1e30
f32 = jnp.float32
bf16 = jnp.bfloat16


def rope_tables(posint, half_dim):
    pair_ids = jnp.arange(half_dim)
    first_cut = half_dim // 4
    second_cut = first_cut + (half_dim - first_cut) // 2
    group_of = (pair_ids >= first_cut).astype(jnp.int32) + (pair_ids >= second_cut).astype(
        jnp.int32
    )
    starts = jnp.where(group_of == 0, 0, jnp.where(group_of == 1, first_cut, second_cut))
    counts = jnp.where(
        group_of == 0,
        first_cut,
        jnp.where(group_of == 1, second_cut - first_cut, half_dim - second_cut),
    )
    frequency = jnp.exp(
        -math.log(10000.0) * (pair_ids - starts).astype(f32) / counts.astype(f32)
    )
    spots = posint.astype(f32)[:, :, None]
    coords = jnp.where(group_of == 0, spots[0], jnp.where(group_of == 1, spots[1], spots[2]))
    angles = coords * frequency[None, :]
    return (jnp.cos(angles), jnp.sin(angles))


def rotate(vector, cos_tab, sin_tab):
    half_dim = cos_tab.shape[-1]
    front = vector[..., :half_dim]
    behind = vector[..., half_dim:]
    return jnp.concatenate(
        [front * cos_tab - behind * sin_tab, front * sin_tab + behind * cos_tab], -1
    )


def rms_norm(vector, eps_value):
    inverse = lax.rsqrt(jnp.mean(vector * vector, -1, keepdims=True) + eps_value)
    return (vector * inverse, inverse)


def norm_back(normed, inverse, gradient):
    return inverse * (gradient - normed * jnp.mean(gradient * normed, -1, keepdims=True))


def timestep_embed(time_step, embed_width):
    half_dim = embed_width // 2
    frequency = jnp.exp(-math.log(10000.0) * jnp.arange(half_dim, dtype=f32) / half_dim)
    angles = time_step.astype(f32)[..., None] * frequency
    return jnp.concatenate([jnp.cos(angles), jnp.sin(angles)], -1)


def dot(a, b):
    return jnp.dot(a, b, preferred_element_type=f32)


def dot_tn(a, b):
    return lax.dot_general(a, b, (((0,), (0,)), ((), ())), preferred_element_type=f32)


def dot_nt(a, b):
    return lax.dot_general(a, b, (((1,), (1,)), ((), ())), preferred_element_type=f32)


def ein(spec, a, b):
    return jnp.einsum(spec, a, b, preferred_element_type=f32)


def make_body(clips, outer, inner):
    shards = clips * outer
    team = "inner"
    spread = ("clip", "outer") if outer > 1 else "clip"
    whole_clip = ("outer", "inner") if outer > 1 else "inner"

    def gather_team(x):
        return lax.all_gather(x, team, axis=0, tiled=True)

    def scatter_team(x):
        return lax.psum_scatter(x, team, scatter_dimension=0, tiled=True)

    def swap_team(x):
        return lax.all_to_all(x, team, split_axis=0, concat_axis=0, tiled=True)

    def gather_spread(x):
        return lax.all_gather(x, spread, axis=0, tiled=True)

    def scatter_spread(x):
        return lax.psum_scatter(x, spread, scatter_dimension=0, tiled=True)

    def by_columns(w):
        rows, columns = w.shape
        blocks = w.reshape(rows, shards, inner, columns // (shards * inner))
        return blocks.transpose(2, 0, 1, 3).reshape(inner, rows, columns // inner)

    def back_columns(w):
        _, rows, columns = w.shape
        blocks = w.reshape(inner, rows, shards, columns // shards)
        return blocks.transpose(1, 2, 0, 3).reshape(rows, inner * columns)

    def body(
        tokens,
        caption,
        lengths,
        timesteps,
        positions,
        w_time,
        w_pool,
        w_ada,
        b_ada,
        norm1_gain,
        w_qkv,
        w_key_text,
        w_value_text,
        cross_gate,
        w_out,
        norm2_gain,
        w_gate,
        w_up,
        w_down,
        cotangent,
    ):
        head_count = cross_gate.shape[0]
        width = tokens.shape[2]
        head_dim = width // head_count
        heads = head_count // inner
        own = heads * head_dim
        tok_rows = tokens.shape[1]
        team_rows = tok_rows * inner
        cap_rows = caption.shape[1]
        cond_width = w_pool.shape[1]
        mod_width = b_ada.shape[0]
        mod_own = mod_width // inner
        attn_scale = 1.0 / math.sqrt(head_dim)
        member = lax.axis_index(team)
        shard = lax.axis_index(spread)
        length_f = lengths[0].astype(f32)

        cap_part = swap_team(by_columns(caption[0])).reshape(inner * cap_rows, -1)
        cap_own = cap_part
        if outer > 1:
            cap_part = lax.all_gather(cap_part, "outer", axis=0, tiled=True)
        cap_len = cap_part.shape[0]
        pool_s = gather_spread(w_pool)
        time_s = gather_spread(w_time)
        rows = w_ada.shape[0]
        ada_blocks = w_ada.reshape(rows, inner, mod_own).transpose(1, 0, 2)
        ada_s = gather_spread(swap_team(ada_blocks).reshape(inner * rows, mod_own))
        rows = w_qkv.shape[0]
        qkv_blocks = w_qkv.reshape(rows, 3, inner, own).transpose(2, 0, 1, 3)
        qkv_blocks = qkv_blocks.reshape(inner, rows, 3 * own)
        qkv_s = gather_spread(swap_team(qkv_blocks).reshape(inner * rows, 3 * own))
        tokens_all = gather_team(tokens[0])
        spots = lax.all_gather(positions[:, 0, :], team, axis=1, tiled=True)
        text_s = gather_spread(jnp.concatenate([w_key_text, w_value_text], -1))
        to_heads = [
            (r, (r % shards) * inner + r // shards) for r in range(shards * inner)
        ]
        from_heads = [(b, a) for a, b in to_heads]
        every = ("clip", "outer", "inner")
        out_s = gather_spread(lax.ppermute(w_out, every, to_heads))
        ffn_blocks = jnp.concatenate([by_columns(w_gate), by_columns(w_up)], -1)
        ffn_s = gather_spread(swap_team(ffn_blocks).reshape(inner * rows, -1))
        down_s = gather_spread(w_down)
        ff_own = down_s.shape[0]
        cot_all = gather_team(cotangent[0])

        cap_mask = (jnp.arange(cap_len) < lengths[0]).astype(f32)
        pooled = jnp.sum(cap_part.astype(f32) * cap_mask[:, None], 0) / length_f
        pooled_b = pooled.astype(bf16)
        time_rows = w_time.shape[0]
        embed_width = time_rows * shards * inner
        time_embed = timestep_embed(timesteps[0], embed_width).astype(bf16)
        time_own = lax.dynamic_index_in_dim(
            time_embed.reshape(shards, inner, time_rows), member, 1, keepdims=False
        ).reshape(1, -1)
        condition = lax.psum(dot(pooled_b[None], pool_s) + dot(time_own, time_s), team)
        cond_b = jax.nn.silu(condition).astype(bf16)
        bias_own = lax.dynamic_slice_in_dim(b_ada, member * mod_own, mod_own)
        modulation = gather_team(dot(cond_b, ada_s)[0] + bias_own)
        scale_attn, gate_attn, scale_ffn, gate_ffn = jnp.split(modulation, 4)
        tanh_attn = jnp.tanh(gate_attn)
        tanh_ffn = jnp.tanh(gate_ffn)
        packed = jnp.concatenate(
            [
                modulation,
                condition[0],
                pooled,
                jnp.full((128,), timesteps[0].astype(f32)),
            ]
        )
        clip_facts = lax.all_gather(packed.reshape(-1, 128), "clip", axis=0).reshape(clips, -1)

        normed_all, _ = rms_norm(tokens_all.astype(f32), epsilon)
        gain1 = norm1_gain * (1.0 + scale_attn)
        mix_in = (normed_all * gain1).astype(bf16)
        qkv_own = dot(mix_in, qkv_s).reshape(team_rows, 3, heads, head_dim).transpose(1, 2, 0, 3)
        cos_tab, sin_tab = rope_tables(spots, head_dim // 2)
        queries_n, inverse_q = rms_norm(qkv_own[0], head_eps)
        keys_n, inverse_k = rms_norm(qkv_own[1], head_eps)
        queries_b = rotate(queries_n, cos_tab, sin_tab).astype(bf16)
        keys_b = rotate(keys_n, cos_tab, sin_tab).astype(bf16)
        values_b = qkv_own[2].astype(bf16)
        if outer > 1:
            keys_b = lax.all_gather(keys_b, "outer", axis=1, tiled=True)
            values_b = lax.all_gather(values_b, "outer", axis=1, tiled=True)
        scores = ein("hqd,hkd->hqk", queries_b, keys_b) * attn_scale
        top = jnp.max(scores, -1, keepdims=True)
        raised = jnp.exp(scores - top)
        total = jnp.sum(raised, -1, keepdims=True)
        self_out = ein("hqk,hkd->hqd", raised.astype(bf16), values_b) / total
        log_sum = top + jnp.log(total)

        text_part = dot(cap_part, text_s).astype(bf16)
        text_part = text_part.reshape(cap_len, 2, inner, own).transpose(2, 0, 1, 3)
        text_own = scatter_team(text_part.reshape(inner * cap_len, 2 * own)).astype(f32)
        text_own = text_own.reshape(cap_len, 2, heads, head_dim).transpose(1, 2, 0, 3)
        text_keys_n, inverse_t = rms_norm(text_own[0], head_eps)
        keys_text_b = text_keys_n.astype(bf16)
        values_text_b = text_own[1].astype(bf16)
        cross_scores = ein("hqd,hkd->hqk", queries_b, keys_text_b) * attn_scale
        cross_scores = jnp.where(cap_mask > 0, cross_scores, big_negative)
        cross_probs = jax.nn.softmax(cross_scores, axis=-1)
        cross_probs_b = cross_probs.astype(bf16)
        cross_out = ein("hqk,hkd->hqd", cross_probs_b, values_text_b)
        gate_own = jnp.tanh(lax.dynamic_slice_in_dim(cross_gate, member * heads, heads))
        gate_t = gate_own[:, None, None]
        mixed = self_out + gate_t * cross_out
        mixed_b = mixed.transpose(1, 0, 2).reshape(team_rows, own).astype(bf16)
        attn_out = scatter_team(dot(mixed_b, out_s).astype(bf16)).astype(f32)

        tokens_f = tokens[0].astype(f32)
        normed1, inverse1 = rms_norm(tokens_f, epsilon)
        resid = tokens_f + tanh_attn * attn_out
        normed2, inverse2 = rms_norm(resid, epsilon)
        gain2 = norm2_gain * (1.0 + scale_ffn)
        ffn_in = gather_team((normed2 * gain2).astype(bf16))
        gate_up = dot(ffn_in, ffn_s)
        gate_pre, up_pre = gate_up[:, :ff_own], gate_up[:, ff_own:]
        sigmoid_g = jax.nn.sigmoid(gate_pre)
        silu_g = gate_pre * sigmoid_g
        hidden_b = (silu_g * up_pre).astype(bf16)
        d_ffn_b = (tanh_ffn * cot_all.astype(f32)).astype(bf16)
        d_hidden = dot_nt(d_ffn_b, down_s)
        silu_slope = sigmoid_g * (1.0 + gate_pre * (1.0 - sigmoid_g))
        d_gate_up = jnp.concatenate(
            [
                (d_hidden * up_pre * silu_slope).astype(bf16),
                (d_hidden * silu_g).astype(bf16),
            ],
            -1,
        )
        d_ffn_in = scatter_team(dot_nt(d_gate_up, ffn_s).astype(bf16)).astype(f32)
        ffn_out = scatter_team(dot(hidden_b, down_s).astype(bf16)).astype(f32)
        mixed_out = (resid + tanh_ffn * ffn_out).astype(bf16)
        d_out = cotangent[0].astype(f32)
        sum_gate_ffn = jnp.sum(d_out * ffn_out, 0)
        sum_down = scatter_spread(dot_tn(hidden_b, d_ffn_b).astype(bf16)).astype(f32)
        sum_ffn = scatter_spread(dot_tn(ffn_in, d_gate_up).astype(bf16))
        sum_ffn = swap_team(sum_ffn.reshape(inner, rows, 2 * ff_own))
        sum_gate = back_columns(sum_ffn[:, :, :ff_own]).astype(f32)
        sum_up = back_columns(sum_ffn[:, :, ff_own:]).astype(f32)

        sum_norm2 = jnp.sum(d_ffn_in * normed2, 0)
        d_resid = d_out + norm_back(normed2, inverse2, d_ffn_in * gain2)
        sum_gate_attn = jnp.sum(d_resid * attn_out, 0)
        d_attn_b = gather_team((tanh_attn * d_resid).astype(bf16))
        grad_out = dot_tn(mixed_b, d_attn_b).astype(bf16)
        sum_out = lax.ppermute(scatter_spread(grad_out), every, from_heads).astype(f32)
        d_mixed = dot_nt(d_attn_b, out_s).reshape(team_rows, heads, head_dim).transpose(1, 0, 2)
        grad_cross = jnp.sum(d_mixed * cross_out, axis=(1, 2)) * (1.0 - gate_own * gate_own)
        d_self_b = d_mixed.astype(bf16)
        d_cross_b = (gate_t * d_mixed).astype(bf16)

        d_cross_probs = ein("hqd,hkd->hqk", d_cross_b, values_text_b)
        d_cross_scores = (
            cross_probs
            * (d_cross_probs - jnp.sum(cross_probs * d_cross_probs, -1, keepdims=True))
        ).astype(bf16)
        d_queries = ein("hqk,hkd->hqd", d_cross_scores, keys_text_b)
        d_text_keys_n = ein("hqk,hqd->hkd", d_cross_scores, queries_b) * attn_scale
        d_text_values = ein("hqk,hqd->hkd", cross_probs_b, d_cross_b)
        if outer > 1:
            d_text_keys_n = lax.psum(d_text_keys_n, "outer")
            d_text_values = lax.psum(d_text_values, "outer")
        d_text_keys = norm_back(text_keys_n, inverse_t, d_text_keys_n)
        text_grads = jnp.stack([d_text_keys, d_text_values]).transpose(2, 0, 1, 3)
        text_grads = text_grads.reshape(cap_len, 2 * own).astype(bf16)
        if outer > 1:
            text_grads = lax.dynamic_slice_in_dim(
                text_grads, lax.axis_index("outer") * inner * cap_rows, inner * cap_rows
            )
        text_rows = text_grads.shape[0]
        text_grads = gather_team(text_grads).reshape(inner, text_rows, 2, own)
        text_grads = text_grads.transpose(1, 2, 0, 3).reshape(text_rows, 2 * width)
        sum_text = scatter_spread(dot_tn(cap_own, text_grads).astype(bf16)).astype(f32)
        d_cap = dot_nt(text_grads, text_s).astype(bf16).reshape(inner, cap_rows, -1)
        d_cap = back_columns(swap_team(d_cap)).astype(f32)

        row_dots = jnp.sum(d_self_b.astype(f32) * self_out, -1, keepdims=True)
        soft_probs = jnp.exp(scores - log_sum)
        d_probs = ein("hqd,hkd->hqk", d_self_b, values_b)
        d_scores_b = (soft_probs * (d_probs - row_dots)).astype(bf16)
        d_queries = (d_queries + ein("hqk,hkd->hqd", d_scores_b, keys_b)) * attn_scale
        d_keys = ein("hqk,hqd->hkd", d_scores_b, queries_b) * attn_scale
        d_values = ein("hqk,hqd->hkd", soft_probs.astype(bf16), d_self_b)
        if outer > 1:
            d_keys = lax.psum_scatter(d_keys, "outer", scatter_dimension=1, tiled=True)
            d_values = lax.psum_scatter(d_values, "outer", scatter_dimension=1, tiled=True)
        d_queries_raw = norm_back(queries_n, inverse_q, rotate(d_queries, cos_tab, -sin_tab))
        d_keys_raw = norm_back(keys_n, inverse_k, rotate(d_keys, cos_tab, -sin_tab))
        d_qkv = jnp.stack([d_queries_raw, d_keys_raw, d_values]).astype(bf16)
        d_qkv = d_qkv.transpose(2, 0, 1, 3).reshape(team_rows, 3 * own)
        d_mix_in = scatter_team(dot_nt(d_qkv, qkv_s).astype(bf16)).astype(f32)
        sum_qkv = scatter_spread(dot_tn(mix_in, d_qkv).astype(bf16))
        sum_qkv = swap_team(sum_qkv.reshape(inner, rows, 3 * own)).reshape(inner, rows, 3, own)
        sum_qkv = sum_qkv.transpose(1, 2, 0, 3).reshape(rows, 3 * width).astype(f32)

        sum_norm1 = jnp.sum(d_mix_in * normed1, 0)
        d_tokens = d_resid + norm_back(normed1, inverse1, d_mix_in * gain1)

        cross_slots = jnp.zeros((128,), f32)
        cross_slots = lax.dynamic_update_slice_in_dim(cross_slots, grad_cross, member * heads, 0)
        sums = jnp.concatenate(
            [sum_norm1, sum_gate_attn, sum_norm2, sum_gate_ffn, cross_slots]
        ).reshape(-1, 128)
        sums = lax.psum(sums, whole_clip)
        sums = lax.all_gather(sums, "clip", axis=0).reshape(clips, -1)
        mods = clip_facts[:, :mod_width].reshape(clips, 4, width)
        at = mod_width
        cond_all = clip_facts[:, at : at + cond_width]
        at += cond_width
        pool_all = clip_facts[:, at : at + pooled.shape[0]]
        steps_all = clip_facts[:, at + pooled.shape[0]]
        token_sums = sums[:, :mod_width].reshape(clips, 4, width)
        grad_norm1 = jnp.sum(token_sums[:, 0] * (1.0 + mods[:, 0]), 0)
        grad_norm2 = jnp.sum(token_sums[:, 2] * (1.0 + mods[:, 2]), 0)
        tanh1, tanh3 = jnp.tanh(mods[:, 1]), jnp.tanh(mods[:, 3])
        d_modulation = jnp.concatenate(
            [
                token_sums[:, 0] * norm1_gain,
                token_sums[:, 1] * (1.0 - tanh1 * tanh1),
                token_sums[:, 2] * norm2_gain,
                token_sums[:, 3] * (1.0 - tanh3 * tanh3),
            ],
            -1,
        )
        grad_bias = jnp.sum(d_modulation, 0)
        grad_cross_gate = jnp.sum(sums[:, mod_width : mod_width + head_count], 0)
        row = shard * inner + member
        ada_rows = w_ada.shape[0]
        cond_rows = lax.dynamic_slice_in_dim(
            jax.nn.silu(cond_all).astype(bf16).astype(f32), row * ada_rows, ada_rows, 1
        )
        sum_ada = jnp.sum(cond_rows[:, :, None] * d_modulation[:, None, :], 0)
        d_mod_clip = lax.dynamic_index_in_dim(d_modulation, lax.axis_index("clip"), 0)
        d_mod_own = lax.dynamic_slice_in_dim(d_mod_clip, member * mod_own, mod_own, 1)
        d_cond_act = lax.psum(dot_nt(d_mod_own.astype(bf16), ada_s), team)
        sigmoid_c = jax.nn.sigmoid(condition)
        d_condition = d_cond_act * sigmoid_c * (1.0 + condition * (1.0 - sigmoid_c))
        d_cond_all = lax.all_gather(d_condition[0], "clip", axis=0)
        d_pooled = gather_team(dot_nt(d_condition.astype(bf16), pool_s)[0])
        d_pooled = d_pooled.reshape(inner, shards, -1).transpose(1, 0, 2).reshape(1, -1)
        seq_row = lax.axis_index(whole_clip)
        local_mask = (seq_row * cap_rows + jnp.arange(cap_rows) < lengths[0]).astype(f32)
        d_caption = d_cap + local_mask[:, None] * d_pooled / length_f
        embed_all = timestep_embed(steps_all, embed_width).astype(bf16).astype(f32)
        embed_rows = lax.dynamic_slice_in_dim(embed_all, row * time_rows, time_rows, 1)
        sum_time = jnp.sum(embed_rows[:, :, None] * d_cond_all[:, None, :], 0)
        pool_rows = lax.dynamic_slice_in_dim(
            pool_all.astype(bf16).astype(f32), shard * w_pool.shape[0], w_pool.shape[0], 1
        )
        sum_pool = jnp.sum(pool_rows[:, :, None] * d_cond_all[:, None, :], 0)
        return (
            mixed_out[None],
            d_tokens[None],
            d_caption[None],
            sum_time,
            sum_pool,
            sum_ada,
            grad_bias,
            grad_norm1,
            sum_qkv,
            sum_text[:, :width],
            sum_text[:, width:],
            grad_cross_gate,
            sum_out,
            grad_norm2,
            sum_gate,
            sum_up,
            sum_down,
        )

    return body


def solution(mesh):
    clips, members = mesh.shape["clip"], mesh.shape["seq"]

    def run(*args):
        inner = math.gcd(args[13].shape[0], members)
        outer = members // inner
        fine = Mesh(mesh.devices.reshape(clips, outer, inner), ("clip", "outer", "inner"))
        seq = ("outer", "inner")
        every = P(("clip", "outer", "inner"), None)
        by_token = P("clip", seq, None)
        return jax.shard_map(
            make_body(clips, outer, inner),
            mesh=fine,
            in_specs=(
                by_token,
                by_token,
                P("clip"),
                P("clip"),
                P(None, "clip", seq),
                every,
                every,
                every,
                P(),
                P(),
                every,
                every,
                every,
                P(),
                every,
                P(),
                every,
                every,
                every,
                by_token,
            ),
            out_specs=(
                by_token,
                by_token,
                by_token,
                every,
                every,
                every,
                P(),
                P(),
                every,
                every,
                every,
                P(),
                every,
                P(),
                every,
                every,
                every,
            ),
            check_vma=False,
        )(*args)

    return run
```

```python
import math

import jax
import jax.numpy as jnp
from jax import lax
from jax.sharding import Mesh
from jax.sharding import PartitionSpec as P

epsilon = 1e-05
head_eps = 1e-06
big_negative = -1e30
f32 = jnp.float32
bf16 = jnp.bfloat16


def rope_tables(posint, half_dim):
    pair_ids = jnp.arange(half_dim)
    first_cut = half_dim // 4
    second_cut = first_cut + (half_dim - first_cut) // 2
    group_of = (pair_ids >= first_cut).astype(jnp.int32) + (pair_ids >= second_cut).astype(
        jnp.int32
    )
    starts = jnp.where(group_of == 0, 0, jnp.where(group_of == 1, first_cut, second_cut))
    counts = jnp.where(
        group_of == 0,
        first_cut,
        jnp.where(group_of == 1, second_cut - first_cut, half_dim - second_cut),
    )
    frequency = jnp.exp(
        -math.log(10000.0) * (pair_ids - starts).astype(f32) / counts.astype(f32)
    )
    spots = posint.astype(f32)[:, :, None]
    coords = jnp.where(group_of == 0, spots[0], jnp.where(group_of == 1, spots[1], spots[2]))
    angles = coords * frequency[None, :]
    return (jnp.cos(angles), jnp.sin(angles))


def rotate(vector, cos_tab, sin_tab):
    half_dim = cos_tab.shape[-1]
    front = vector[..., :half_dim]
    behind = vector[..., half_dim:]
    return jnp.concatenate(
        [front * cos_tab - behind * sin_tab, front * sin_tab + behind * cos_tab], -1
    )


def rms_norm(vector, eps_value):
    inverse = lax.rsqrt(jnp.mean(vector * vector, -1, keepdims=True) + eps_value)
    return (vector * inverse, inverse)


def norm_back(normed, inverse, gradient):
    return inverse * (gradient - normed * jnp.mean(gradient * normed, -1, keepdims=True))


def timestep_embed(time_step, embed_width):
    half_dim = embed_width // 2
    frequency = jnp.exp(-math.log(10000.0) * jnp.arange(half_dim, dtype=f32) / half_dim)
    angles = time_step.astype(f32)[..., None] * frequency
    return jnp.concatenate([jnp.cos(angles), jnp.sin(angles)], -1)


def dot(a, b):
    return jnp.dot(a, b, preferred_element_type=f32)


def dot_tn(a, b):
    return lax.dot_general(a, b, (((0,), (0,)), ((), ())), preferred_element_type=f32)


def dot_nt(a, b):
    return lax.dot_general(a, b, (((1,), (1,)), ((), ())), preferred_element_type=f32)


def ein(spec, a, b):
    return jnp.einsum(spec, a, b, preferred_element_type=f32)


def make_body(clips, outer, ring, pair):
    inner = ring * pair
    shards = clips * outer
    team = ("ring", "pair")
    spread = ("clip", "outer") if outer > 1 else "clip"
    spread_ffn = ("clip", "outer", "pair")
    every = ("clip", "outer", "ring", "pair")
    forward = [(z, (z + 1) % ring) for z in range(ring)]
    crossed = [(x, (x + 1) % pair) for x in range(pair)]
    slots = [(k, e) for k in range(ring) for e in range(pair)]

    def swap_team(x):
        return lax.all_to_all(x, team, split_axis=0, concat_axis=0, tiled=True)

    def gather_spread(x, axes=spread):
        return lax.all_gather(x, axes, axis=0, tiled=True)

    def scatter_spread(x, axes=spread):
        return lax.psum_scatter(x, axes, scatter_dimension=0, tiled=True)

    def ring_gather(x):
        parts, now = [], x
        for k in range(ring):
            parts.append(now)
            other = now
            for _ in range(1, pair):
                other = lax.ppermute(other, "pair", crossed)
                parts.append(other)
            if k + 1 < ring:
                now = lax.ppermute(now, "ring", forward)
        return parts

    def ring_scatter(block_of):
        passed = None
        for step in range(1, ring + 1):
            k = step % ring
            total = block_of(k, 0).astype(f32)
            if pair > 1:
                total = total + lax.ppermute(block_of(k, 1), "pair", crossed).astype(f32)
            if passed is not None:
                total = total + passed.astype(f32)
            if step < ring:
                passed = lax.ppermute(total.astype(bf16), "ring", forward)
        return total

    def row_blocks(x):
        rows = x.shape[0] // inner
        return lambda k, e: x[(k * pair + e) * rows : (k * pair + e + 1) * rows]

    def line_gather(x):
        parts = [x]
        for _ in range(1, ring):
            parts.append(lax.ppermute(parts[-1], "ring", forward))
        return jnp.concatenate(parts, 0)

    def line_scatter(x):
        rows = x.shape[0] // ring
        passed = None
        for step in range(1, ring + 1):
            k = step % ring
            total = x[k * rows : (k + 1) * rows].astype(f32)
            if passed is not None:
                total = total + passed.astype(f32)
            if step < ring:
                passed = lax.ppermute(total.astype(bf16), "ring", forward)
        return total

    def direct(x, k, e):
        if k == 0 and e == 0:
            return x
        moves = [
            (z * pair + y, (z + k) % ring * pair + (y + e) % pair)
            for z in range(ring)
            for y in range(pair)
        ]
        return lax.ppermute(x, team, moves)

    def small_gather(x):
        return [direct(x, k, e) for k, e in slots]

    def small_sum(x):
        parts = small_gather(x)
        total = parts[0]
        for part in parts[1:]:
            total = total + part
        return total

    def in_order(parts):
        z, y = lax.axis_index("ring"), lax.axis_index("pair")
        whole = jnp.zeros((inner,) + parts[0].shape, parts[0].dtype)
        for (k, e), part in zip(slots, parts):
            spot = lax.rem(z + ring - k, ring) * pair + lax.rem(y + pair - e, pair)
            whole = lax.dynamic_update_index_in_dim(whole, part, spot, 0)
        return whole

    def slot_blocks(x):
        z, y = lax.axis_index("ring"), lax.axis_index("pair")

        def block_of(k, e):
            spot = lax.rem(z + ring - k, ring) * pair + lax.rem(y + pair - e, pair)
            return lax.dynamic_index_in_dim(x, spot, 0, keepdims=False)

        return block_of

    def by_columns(w):
        rows, columns = w.shape
        blocks = w.reshape(rows, shards, inner, columns // (shards * inner))
        return blocks.transpose(2, 0, 1, 3).reshape(inner, rows, columns // inner)

    def back_columns(w):
        _, rows, columns = w.shape
        blocks = w.reshape(inner, rows, shards, columns // shards)
        return blocks.transpose(1, 2, 0, 3).reshape(rows, inner * columns)

    def line_columns(w):
        rows, columns = w.shape
        blocks = w.reshape(rows, shards, ring, columns // (shards * ring))
        return blocks.transpose(2, 0, 1, 3).reshape(ring, rows, columns // ring)

    def back_line_columns(w):
        _, rows, columns = w.shape
        blocks = w.reshape(ring, rows, shards, columns // shards)
        return blocks.transpose(1, 2, 0, 3).reshape(rows, ring * columns)

    def body(
        tokens,
        caption,
        lengths,
        timesteps,
        positions,
        w_time,
        w_pool,
        w_ada,
        b_ada,
        norm1_gain,
        w_qkv,
        w_key_text,
        w_value_text,
        cross_gate,
        w_out,
        norm2_gain,
        w_gate,
        w_up,
        w_down,
        cotangent,
    ):
        head_count = cross_gate.shape[0]
        width = tokens.shape[2]
        head_dim = width // head_count
        heads = head_count // inner
        own = heads * head_dim
        tok_rows = tokens.shape[1]
        team_rows = tok_rows * inner
        cap_rows = caption.shape[1]
        cond_width = w_pool.shape[1]
        mod_width = b_ada.shape[0]
        mod_own = mod_width // inner
        attn_scale = 1.0 / math.sqrt(head_dim)
        member = lax.axis_index(team)
        shard = lax.axis_index(spread)
        length_f = lengths[0].astype(f32)

        cap_part = swap_team(by_columns(caption[0])).reshape(inner * cap_rows, -1)
        cap_own = cap_part
        if outer > 1:
            cap_part = lax.all_gather(cap_part, "outer", axis=0, tiled=True)
        cap_len = cap_part.shape[0]
        pool_s = gather_spread(w_pool)
        time_s = gather_spread(w_time)
        rows = w_ada.shape[0]
        ada_blocks = w_ada.reshape(rows, inner, mod_own).transpose(1, 0, 2)
        ada_s = gather_spread(swap_team(ada_blocks).reshape(inner * rows, mod_own))
        rows = w_qkv.shape[0]
        qkv_blocks = w_qkv.reshape(rows, 3, inner, own).transpose(2, 0, 1, 3)
        qkv_blocks = qkv_blocks.reshape(inner, rows, 3 * own)
        qkv_s = gather_spread(swap_team(qkv_blocks).reshape(inner * rows, 3 * own))
        tokens_all = jnp.concatenate(ring_gather(tokens[0]), 0)
        spots = jnp.concatenate(small_gather(positions[:, 0, :].astype(f32)), 1)
        text_s = gather_spread(jnp.concatenate([w_key_text, w_value_text], -1))
        to_heads = [
            (r, (r % shards) * inner + r // shards) for r in range(shards * inner)
        ]
        from_heads = [(b, a) for a, b in to_heads]
        out_s = gather_spread(lax.ppermute(w_out, every, to_heads))
        ffn_blocks = jnp.concatenate([line_columns(w_gate), line_columns(w_up)], -1)
        ffn_blocks = lax.all_to_all(ffn_blocks, "ring", split_axis=0, concat_axis=0, tiled=True)
        ffn_s = gather_spread(ffn_blocks.reshape(ring * rows, -1), spread_ffn)
        ffn_s = ffn_s.reshape(shards, pair, ring, rows, -1).transpose(0, 2, 1, 3, 4)
        ffn_s = ffn_s.reshape(width, -1)
        down_s = gather_spread(w_down, spread_ffn)
        ff_own = down_s.shape[0]
        cot_all = line_gather(cotangent[0])

        cap_mask = (jnp.arange(cap_len) < lengths[0]).astype(f32)
        pooled = jnp.sum(cap_part.astype(f32) * cap_mask[:, None], 0) / length_f
        pooled_b = pooled.astype(bf16)
        time_rows = w_time.shape[0]
        embed_width = time_rows * shards * inner
        time_embed = timestep_embed(timesteps[0], embed_width).astype(bf16)
        time_own = lax.dynamic_index_in_dim(
            time_embed.reshape(shards, inner, time_rows), member, 1, keepdims=False
        ).reshape(1, -1)
        condition = small_sum(dot(pooled_b[None], pool_s) + dot(time_own, time_s))
        cond_b = jax.nn.silu(condition).astype(bf16)
        bias_own = lax.dynamic_slice_in_dim(b_ada, member * mod_own, mod_own)
        modulation = in_order(small_gather(dot(cond_b, ada_s)[0] + bias_own)).reshape(-1)
        scale_attn, gate_attn, scale_ffn, gate_ffn = jnp.split(modulation, 4)
        tanh_attn = jnp.tanh(gate_attn)
        tanh_ffn = jnp.tanh(gate_ffn)
        packed = jnp.concatenate(
            [
                modulation,
                condition[0],
                pooled,
                jnp.full((128,), timesteps[0].astype(f32)),
            ]
        )
        clip_facts = lax.all_gather(packed.reshape(-1, 128), "clip", axis=0).reshape(clips, -1)

        normed_all, _ = rms_norm(tokens_all.astype(f32), epsilon)
        gain1 = norm1_gain * (1.0 + scale_attn)
        mix_in = (normed_all * gain1).astype(bf16)
        qkv_own = dot(mix_in, qkv_s).reshape(team_rows, 3, heads, head_dim).transpose(1, 2, 0, 3)
        cos_tab, sin_tab = rope_tables(spots, head_dim // 2)
        queries_n, inverse_q = rms_norm(qkv_own[0], head_eps)
        keys_n, inverse_k = rms_norm(qkv_own[1], head_eps)
        queries_b = rotate(queries_n, cos_tab, sin_tab).astype(bf16)
        keys_b = rotate(keys_n, cos_tab, sin_tab).astype(bf16)
        values_b = qkv_own[2].astype(bf16)
        if outer > 1:
            keys_b = lax.all_gather(keys_b, "outer", axis=1, tiled=True)
            values_b = lax.all_gather(values_b, "outer", axis=1, tiled=True)
        scores = ein("hqd,hkd->hqk", queries_b, keys_b) * attn_scale
        top = jnp.max(scores, -1, keepdims=True)
        raised = jnp.exp(scores - top)
        total = jnp.sum(raised, -1, keepdims=True)
        self_out = ein("hqk,hkd->hqd", raised.astype(bf16), values_b) / total
        log_sum = top + jnp.log(total)

        text_part = dot(cap_part, text_s).astype(bf16)
        text_part = text_part.reshape(cap_len, 2, inner, own).transpose(2, 0, 1, 3)
        text_own = ring_scatter(slot_blocks(text_part.reshape(inner, cap_len, 2 * own)))
        text_own = text_own.reshape(cap_len, 2, heads, head_dim).transpose(1, 2, 0, 3)
        text_keys_n, inverse_t = rms_norm(text_own[0], head_eps)
        keys_text_b = text_keys_n.astype(bf16)
        values_text_b = text_own[1].astype(bf16)
        cross_scores = ein("hqd,hkd->hqk", queries_b, keys_text_b) * attn_scale
        cross_scores = jnp.where(cap_mask > 0, cross_scores, big_negative)
        cross_probs = jax.nn.softmax(cross_scores, axis=-1)
        cross_probs_b = cross_probs.astype(bf16)
        cross_out = ein("hqk,hkd->hqd", cross_probs_b, values_text_b)
        gate_own = jnp.tanh(lax.dynamic_slice_in_dim(cross_gate, member * heads, heads))
        gate_t = gate_own[:, None, None]
        mixed = self_out + gate_t * cross_out
        mixed_b = mixed.transpose(1, 0, 2).reshape(team_rows, own).astype(bf16)
        attn_out = ring_scatter(row_blocks(dot(mixed_b, out_s).astype(bf16)))

        tokens_f = tokens[0].astype(f32)
        normed1, inverse1 = rms_norm(tokens_f, epsilon)
        resid = tokens_f + tanh_attn * attn_out
        normed2, inverse2 = rms_norm(resid, epsilon)
        gain2 = norm2_gain * (1.0 + scale_ffn)
        ffn_in = line_gather((normed2 * gain2).astype(bf16))
        gate_up = dot(ffn_in, ffn_s)
        gate_pre, up_pre = gate_up[:, :ff_own], gate_up[:, ff_own:]
        sigmoid_g = jax.nn.sigmoid(gate_pre)
        silu_g = gate_pre * sigmoid_g
        hidden_b = (silu_g * up_pre).astype(bf16)
        d_ffn_b = (tanh_ffn * cot_all.astype(f32)).astype(bf16)
        d_hidden = dot_nt(d_ffn_b, down_s)
        silu_slope = sigmoid_g * (1.0 + gate_pre * (1.0 - sigmoid_g))
        d_gate_up = jnp.concatenate(
            [
                (d_hidden * up_pre * silu_slope).astype(bf16),
                (d_hidden * silu_g).astype(bf16),
            ],
            -1,
        )
        d_ffn_in = line_scatter(dot_nt(d_gate_up, ffn_s).astype(bf16))
        ffn_out = line_scatter(dot(hidden_b, down_s).astype(bf16))
        mixed_out = (resid + tanh_ffn * ffn_out).astype(bf16)
        d_out = cotangent[0].astype(f32)
        sum_gate_ffn = jnp.sum(d_out * ffn_out, 0)
        grad_down = dot_tn(hidden_b, d_ffn_b).astype(bf16)
        sum_down = scatter_spread(grad_down, spread_ffn).astype(f32)
        grad_ffn = dot_tn(ffn_in, d_gate_up).astype(bf16)
        grad_ffn = grad_ffn.reshape(shards, ring, pair, rows, -1).transpose(0, 2, 1, 3, 4)
        sum_ffn = scatter_spread(grad_ffn.reshape(width, -1), spread_ffn)
        sum_ffn = sum_ffn.reshape(ring, rows, 2 * ff_own)
        sum_ffn = lax.all_to_all(sum_ffn, "ring", split_axis=0, concat_axis=0, tiled=True)
        sum_gate = back_line_columns(sum_ffn[:, :, :ff_own]).astype(f32)
        sum_up = back_line_columns(sum_ffn[:, :, ff_own:]).astype(f32)

        sum_norm2 = jnp.sum(d_ffn_in * normed2, 0)
        d_resid = d_out + norm_back(normed2, inverse2, d_ffn_in * gain2)
        sum_gate_attn = jnp.sum(d_resid * attn_out, 0)
        d_attn_b = jnp.concatenate(ring_gather((tanh_attn * d_resid).astype(bf16)), 0)
        grad_out = dot_tn(mixed_b, d_attn_b).astype(bf16)
        sum_out = lax.ppermute(scatter_spread(grad_out), every, from_heads).astype(f32)
        d_mixed = dot_nt(d_attn_b, out_s).reshape(team_rows, heads, head_dim).transpose(1, 0, 2)
        grad_cross = jnp.sum(d_mixed * cross_out, axis=(1, 2)) * (1.0 - gate_own * gate_own)
        d_self_b = d_mixed.astype(bf16)
        d_cross_b = (gate_t * d_mixed).astype(bf16)

        d_cross_probs = ein("hqd,hkd->hqk", d_cross_b, values_text_b)
        d_cross_scores = (
            cross_probs
            * (d_cross_probs - jnp.sum(cross_probs * d_cross_probs, -1, keepdims=True))
        ).astype(bf16)
        d_queries = ein("hqk,hkd->hqd", d_cross_scores, keys_text_b)
        d_text_keys_n = ein("hqk,hqd->hkd", d_cross_scores, queries_b) * attn_scale
        d_text_values = ein("hqk,hqd->hkd", cross_probs_b, d_cross_b)
        if outer > 1:
            d_text_keys_n = lax.psum(d_text_keys_n, "outer")
            d_text_values = lax.psum(d_text_values, "outer")
        d_text_keys = norm_back(text_keys_n, inverse_t, d_text_keys_n)
        text_grads = jnp.stack([d_text_keys, d_text_values]).transpose(2, 0, 1, 3)
        text_grads = text_grads.reshape(cap_len, 2 * own).astype(bf16)
        if outer > 1:
            text_grads = lax.dynamic_slice_in_dim(
                text_grads, lax.axis_index("outer") * inner * cap_rows, inner * cap_rows
            )
        text_rows = text_grads.shape[0]
        text_grads = in_order(ring_gather(text_grads)).reshape(inner, text_rows, 2, own)
        text_grads = text_grads.transpose(1, 2, 0, 3).reshape(text_rows, 2 * width)
        sum_text = scatter_spread(dot_tn(cap_own, text_grads).astype(bf16)).astype(f32)
        d_cap = dot_nt(text_grads, text_s).astype(bf16).reshape(inner, cap_rows, -1)
        d_cap = back_columns(swap_team(d_cap)).astype(f32)

        row_dots = jnp.sum(d_self_b.astype(f32) * self_out, -1, keepdims=True)
        soft_probs = jnp.exp(scores - log_sum)
        d_probs = ein("hqd,hkd->hqk", d_self_b, values_b)
        d_scores_b = (soft_probs * (d_probs - row_dots)).astype(bf16)
        d_queries = (d_queries + ein("hqk,hkd->hqd", d_scores_b, keys_b)) * attn_scale
        d_keys = ein("hqk,hqd->hkd", d_scores_b, queries_b) * attn_scale
        d_values = ein("hqk,hqd->hkd", soft_probs.astype(bf16), d_self_b)
        if outer > 1:
            d_keys = lax.psum_scatter(d_keys, "outer", scatter_dimension=1, tiled=True)
            d_values = lax.psum_scatter(d_values, "outer", scatter_dimension=1, tiled=True)
        d_queries_raw = norm_back(queries_n, inverse_q, rotate(d_queries, cos_tab, -sin_tab))
        d_keys_raw = norm_back(keys_n, inverse_k, rotate(d_keys, cos_tab, -sin_tab))
        d_qkv = jnp.stack([d_queries_raw, d_keys_raw, d_values]).astype(bf16)
        d_qkv = d_qkv.transpose(2, 0, 1, 3).reshape(team_rows, 3 * own)
        d_mix_in = ring_scatter(row_blocks(dot_nt(d_qkv, qkv_s).astype(bf16)))
        sum_qkv = scatter_spread(dot_tn(mix_in, d_qkv).astype(bf16))
        sum_qkv = swap_team(sum_qkv.reshape(inner, rows, 3 * own)).reshape(inner, rows, 3, own)
        sum_qkv = sum_qkv.transpose(1, 2, 0, 3).reshape(rows, 3 * width).astype(f32)

        sum_norm1 = jnp.sum(d_mix_in * normed1, 0)
        d_tokens = d_resid + norm_back(normed1, inverse1, d_mix_in * gain1)

        cross_slots = jnp.zeros((128,), f32)
        cross_slots = lax.dynamic_update_slice_in_dim(cross_slots, grad_cross, member * heads, 0)
        early = jnp.concatenate([sum_gate_attn, sum_norm2, sum_gate_ffn, cross_slots])
        early = small_sum(early.reshape(-1, 128))
        late = small_sum(sum_norm1.reshape(-1, 128))
        if outer > 1:
            early = lax.psum(early, "outer")
            late = lax.psum(late, "outer")
        early = lax.all_gather(early, "clip", axis=0).reshape(clips, -1)
        late = lax.all_gather(late, "clip", axis=0).reshape(clips, -1)
        sums = jnp.concatenate([late, early], -1)
        mods = clip_facts[:, :mod_width].reshape(clips, 4, width)
        at = mod_width
        cond_all = clip_facts[:, at : at + cond_width]
        at += cond_width
        pool_all = clip_facts[:, at : at + pooled.shape[0]]
        steps_all = clip_facts[:, at + pooled.shape[0]]
        token_sums = sums[:, :mod_width].reshape(clips, 4, width)
        grad_norm1 = jnp.sum(token_sums[:, 0] * (1.0 + mods[:, 0]), 0)
        grad_norm2 = jnp.sum(token_sums[:, 2] * (1.0 + mods[:, 2]), 0)
        tanh1, tanh3 = jnp.tanh(mods[:, 1]), jnp.tanh(mods[:, 3])
        d_modulation = jnp.concatenate(
            [
                token_sums[:, 0] * norm1_gain,
                token_sums[:, 1] * (1.0 - tanh1 * tanh1),
                token_sums[:, 2] * norm2_gain,
                token_sums[:, 3] * (1.0 - tanh3 * tanh3),
            ],
            -1,
        )
        grad_bias = jnp.sum(d_modulation, 0)
        grad_cross_gate = jnp.sum(sums[:, mod_width : mod_width + head_count], 0)
        row = shard * inner + member
        ada_rows = w_ada.shape[0]
        cond_rows = lax.dynamic_slice_in_dim(
            jax.nn.silu(cond_all).astype(bf16).astype(f32), row * ada_rows, ada_rows, 1
        )
        sum_ada = jnp.sum(cond_rows[:, :, None] * d_modulation[:, None, :], 0)
        d_mod_clip = lax.dynamic_index_in_dim(d_modulation, lax.axis_index("clip"), 0)
        d_mod_own = lax.dynamic_slice_in_dim(d_mod_clip, member * mod_own, mod_own, 1)
        d_cond_act = small_sum(dot_nt(d_mod_own.astype(bf16), ada_s))
        sigmoid_c = jax.nn.sigmoid(condition)
        d_condition = d_cond_act * sigmoid_c * (1.0 + condition * (1.0 - sigmoid_c))
        d_cond_all = lax.all_gather(d_condition[0], "clip", axis=0)
        d_pooled = in_order(small_gather(dot_nt(d_condition.astype(bf16), pool_s)[0]))
        d_pooled = d_pooled.reshape(inner, shards, -1).transpose(1, 0, 2).reshape(1, -1)
        seq_row = lax.axis_index(("outer", "ring", "pair"))
        local_mask = (seq_row * cap_rows + jnp.arange(cap_rows) < lengths[0]).astype(f32)
        d_caption = d_cap + local_mask[:, None] * d_pooled / length_f
        embed_all = timestep_embed(steps_all, embed_width).astype(bf16).astype(f32)
        embed_rows = lax.dynamic_slice_in_dim(embed_all, row * time_rows, time_rows, 1)
        sum_time = jnp.sum(embed_rows[:, :, None] * d_cond_all[:, None, :], 0)
        pool_rows = lax.dynamic_slice_in_dim(
            pool_all.astype(bf16).astype(f32), shard * w_pool.shape[0], w_pool.shape[0], 1
        )
        sum_pool = jnp.sum(pool_rows[:, :, None] * d_cond_all[:, None, :], 0)
        return (
            mixed_out[None],
            d_tokens[None],
            d_caption[None],
            sum_time,
            sum_pool,
            sum_ada,
            grad_bias,
            grad_norm1,
            sum_qkv,
            sum_text[:, :width],
            sum_text[:, width:],
            grad_cross_gate,
            sum_out,
            grad_norm2,
            sum_gate,
            sum_up,
            sum_down,
        )

    return body


def solution(mesh):
    clips, members = mesh.shape["clip"], mesh.shape["seq"]

    def run(*args):
        inner = math.gcd(args[13].shape[0], members)
        outer, pair = members // inner, math.gcd(inner, 2)
        ring = inner // pair
        names = ("clip", "outer", "ring", "pair")
        fine = Mesh(mesh.devices.reshape(clips, outer, ring, pair), names)
        seq = names[1:]
        every = P(names, None)
        by_token = P("clip", seq, None)
        return jax.shard_map(
            make_body(clips, outer, ring, pair),
            mesh=fine,
            in_specs=(
                by_token,
                by_token,
                P("clip"),
                P("clip"),
                P(None, "clip", seq),
                every,
                every,
                every,
                P(),
                P(),
                every,
                every,
                every,
                P(),
                every,
                P(),
                every,
                every,
                every,
                by_token,
            ),
            out_specs=(
                by_token,
                by_token,
                by_token,
                every,
                every,
                every,
                P(),
                P(),
                every,
                every,
                every,
                P(),
                every,
                P(),
                every,
                every,
                every,
            ),
            check_vma=False,
        )(*args)

    return run
```

```python
import math

import jax
import jax.numpy as jnp
from jax import lax
from jax.sharding import Mesh
from jax.sharding import PartitionSpec as P

epsilon = 1e-05
head_eps = 1e-06
big_negative = -1e30
f32 = jnp.float32
bf16 = jnp.bfloat16


def rope_tables(posint, half_dim):
    pair_ids = jnp.arange(half_dim)
    first_cut = half_dim // 4
    second_cut = first_cut + (half_dim - first_cut) // 2
    group_of = (pair_ids >= first_cut).astype(jnp.int32) + (pair_ids >= second_cut).astype(
        jnp.int32
    )
    starts = jnp.where(group_of == 0, 0, jnp.where(group_of == 1, first_cut, second_cut))
    counts = jnp.where(
        group_of == 0,
        first_cut,
        jnp.where(group_of == 1, second_cut - first_cut, half_dim - second_cut),
    )
    frequency = jnp.exp(
        -math.log(10000.0) * (pair_ids - starts).astype(f32) / counts.astype(f32)
    )
    spots = posint.astype(f32)[:, :, None]
    coords = jnp.where(group_of == 0, spots[0], jnp.where(group_of == 1, spots[1], spots[2]))
    angles = coords * frequency[None, :]
    return (jnp.cos(angles), jnp.sin(angles))


def rotate(vector, cos_tab, sin_tab):
    half_dim = cos_tab.shape[-1]
    front = vector[..., :half_dim]
    behind = vector[..., half_dim:]
    return jnp.concatenate(
        [front * cos_tab - behind * sin_tab, front * sin_tab + behind * cos_tab], -1
    )


def rms_norm(vector, eps_value):
    inverse = lax.rsqrt(jnp.mean(vector * vector, -1, keepdims=True) + eps_value)
    return (vector * inverse, inverse)


def norm_back(normed, inverse, gradient):
    return inverse * (gradient - normed * jnp.mean(gradient * normed, -1, keepdims=True))


def timestep_embed(time_step, embed_width):
    half_dim = embed_width // 2
    frequency = jnp.exp(-math.log(10000.0) * jnp.arange(half_dim, dtype=f32) / half_dim)
    angles = time_step.astype(f32)[..., None] * frequency
    return jnp.concatenate([jnp.cos(angles), jnp.sin(angles)], -1)


def dot(a, b):
    return jnp.dot(a, b, preferred_element_type=f32)


def dot_tn(a, b):
    return lax.dot_general(a, b, (((0,), (0,)), ((), ())), preferred_element_type=f32)


def dot_nt(a, b):
    return lax.dot_general(a, b, (((1,), (1,)), ((), ())), preferred_element_type=f32)


def ein(spec, a, b):
    return jnp.einsum(spec, a, b, preferred_element_type=f32)


def tie(*arrays):
    return lax.optimization_barrier(arrays)


def make_body(clips, outer, ring, pair):
    inner = ring * pair
    shards = clips * outer
    team = ("ring", "pair")
    spread = ("clip", "outer") if outer > 1 else "clip"
    spread_ffn = ("clip", "outer", "pair")
    every = ("clip", "outer", "ring", "pair")
    forward = [(z, (z + 1) % ring) for z in range(ring)]
    crossed = [(x, (x + 1) % pair) for x in range(pair)]
    slots = [(k, e) for k in range(ring) for e in range(pair)]

    def swap_team(x):
        return lax.all_to_all(x, team, split_axis=0, concat_axis=0, tiled=True)

    def gather_spread(x, axes=spread):
        return lax.all_gather(x, axes, axis=0, tiled=True)

    def scatter_spread(x, axes=spread):
        return lax.psum_scatter(x, axes, scatter_dimension=0, tiled=True)

    def ring_gather(x):
        parts, now = [], x
        for k in range(ring):
            parts.append(now)
            other = now
            for _ in range(1, pair):
                other = lax.ppermute(other, "pair", crossed)
                parts.append(other)
            if k + 1 < ring:
                now = lax.ppermute(now, "ring", forward)
        return parts

    def ring_scatter(block_of):
        passed = None
        for step in range(1, ring + 1):
            k = step % ring
            total = block_of(k, 0).astype(f32)
            if pair > 1:
                total = total + lax.ppermute(block_of(k, 1), "pair", crossed).astype(f32)
            if passed is not None:
                total = total + passed.astype(f32)
            if step < ring:
                passed = lax.ppermute(total.astype(bf16), "ring", forward)
        return total

    def row_blocks(x):
        rows = x.shape[0] // inner
        return lambda k, e: x[(k * pair + e) * rows : (k * pair + e + 1) * rows]

    def line_gather(x):
        parts = [x]
        for _ in range(1, ring):
            parts.append(lax.ppermute(parts[-1], "ring", forward))
        return jnp.concatenate(parts, 0)

    def line_scatter(x):
        rows = x.shape[0] // ring
        passed = None
        for step in range(1, ring + 1):
            k = step % ring
            total = x[k * rows : (k + 1) * rows].astype(f32)
            if passed is not None:
                total = total + passed.astype(f32)
            if step < ring:
                passed = lax.ppermute(total.astype(bf16), "ring", forward)
        return total

    def small_sum(x):
        for axis, size in (("pair", pair), ("ring", ring)):
            if size & (size - 1):
                x = lax.psum(x, axis)
                continue
            hop = 1
            while hop < size:
                x = x + lax.ppermute(x, axis, [(i, i ^ hop) for i in range(size)])
                hop *= 2
        return x

    def small_gather(x):
        return swap_team(jnp.broadcast_to(x, (inner,) + x.shape))

    def in_order(parts):
        z, y = lax.axis_index("ring"), lax.axis_index("pair")
        if pair > 1:
            front = [jnp.where(y == 0, parts[2 * k], parts[2 * k + 1]) for k in range(ring)]
            behind = [jnp.where(y == 0, parts[2 * k + 1], parts[2 * k]) for k in range(ring)]
            rows = [jnp.stack([f, g]) for f, g in zip(front, behind)]
        else:
            rows = [part[None] for part in parts]
        twice = jnp.stack((rows[1:] + rows)[::-1])
        whole = lax.dynamic_slice_in_dim(twice, ring - 1 - z, ring)
        return whole.reshape((inner,) + parts[0].shape)

    def slot_blocks(x):
        z, y = lax.axis_index("ring"), lax.axis_index("pair")

        def block_of(k, e):
            spot = lax.rem(z + ring - k, ring) * pair + lax.rem(y + pair - e, pair)
            return lax.dynamic_index_in_dim(x, spot, 0, keepdims=False)

        return block_of

    def by_columns(w):
        rows, columns = w.shape
        blocks = w.reshape(rows, shards, inner, columns // (shards * inner))
        return blocks.transpose(2, 0, 1, 3).reshape(inner, rows, columns // inner)

    def back_columns(w):
        _, rows, columns = w.shape
        blocks = w.reshape(inner, rows, shards, columns // shards)
        return blocks.transpose(1, 2, 0, 3).reshape(rows, inner * columns)

    def line_columns(w):
        rows, columns = w.shape
        blocks = w.reshape(rows, shards, ring, columns // (shards * ring))
        return blocks.transpose(2, 0, 1, 3).reshape(ring, rows, columns // ring)

    def back_line_columns(w):
        _, rows, columns = w.shape
        blocks = w.reshape(ring, rows, shards, columns // shards)
        return blocks.transpose(1, 2, 0, 3).reshape(rows, ring * columns)

    def body(
        tokens,
        caption,
        lengths,
        timesteps,
        positions,
        w_time,
        w_pool,
        w_ada,
        b_ada,
        norm1_gain,
        w_qkv,
        w_key_text,
        w_value_text,
        cross_gate,
        w_out,
        norm2_gain,
        w_gate,
        w_up,
        w_down,
        cotangent,
    ):
        head_count = cross_gate.shape[0]
        width = tokens.shape[2]
        head_dim = width // head_count
        heads = head_count // inner
        own = heads * head_dim
        tok_rows = tokens.shape[1]
        team_rows = tok_rows * inner
        cap_rows = caption.shape[1]
        cond_width = w_pool.shape[1]
        mod_width = b_ada.shape[0]
        attn_scale = 1.0 / math.sqrt(head_dim)
        member = lax.axis_index(team)
        shard = lax.axis_index(spread)
        length_f = lengths[0].astype(f32)

        cap_blocks = by_columns(caption[0])
        cap_part = swap_team(cap_blocks).reshape(inner * cap_rows, -1)
        cap_own = cap_part
        if outer > 1:
            cap_part = lax.all_gather(cap_part, "outer", axis=0, tiled=True)
        cap_len = cap_part.shape[0]
        pool_rows, time_rows, ada_rows = w_pool.shape[0], w_time.shape[0], w_ada.shape[0]
        pool_s = gather_spread(jnp.concatenate([w_pool, w_time], 0))
        ada_s = gather_spread(w_ada)
        rows = w_qkv.shape[0]
        qkv_blocks = w_qkv.reshape(rows, 3, inner, own).transpose(2, 0, 1, 3)
        qkv_blocks = qkv_blocks.reshape(inner, rows, 3 * own)
        qkv_s = gather_spread(swap_team(qkv_blocks).reshape(inner * rows, 3 * own))
        spots = positions[:, 0, :].astype(bf16).T
        spots = jnp.concatenate([spots, jnp.zeros((tok_rows, 125), bf16)], -1)
        tokens_all = jnp.concatenate(
            ring_gather(jnp.concatenate([tokens[0], spots], -1)), 0
        )
        spots = tokens_all[:, width : width + 3].astype(f32).T
        tokens_all = tokens_all[:, :width]
        to_heads = [
            (r, (r % shards) * inner + r // shards) for r in range(shards * inner)
        ]
        from_heads = [(b, a) for a, b in to_heads]
        out_rows = lax.ppermute(w_out, every, to_heads)
        text_rows = w_key_text.shape[0]

        cap_mask = (jnp.arange(cap_len) < lengths[0]).astype(f32)
        pooled = jnp.sum(cap_part.astype(f32) * cap_mask[:, None], 0) / length_f
        pooled_b = pooled.astype(bf16)
        embed_width = time_rows * shards * inner
        time_embed = timestep_embed(timesteps[0], embed_width).astype(bf16)
        time_own = lax.dynamic_index_in_dim(
            time_embed.reshape(shards, inner, time_rows), member, 1, keepdims=False
        )
        facts = jnp.concatenate([pooled_b.reshape(shards, pool_rows), time_own], 1)
        condition = small_sum(dot(facts.reshape(1, -1), pool_s))
        cond_b = jax.nn.silu(condition).astype(bf16)
        cond_own = lax.dynamic_index_in_dim(
            cond_b.reshape(shards, inner, ada_rows), member, 1, keepdims=False
        ).reshape(1, -1)
        modulation = small_sum(dot(cond_own, ada_s)).reshape(-1) + b_ada
        scale_attn, gate_attn, scale_ffn, gate_ffn = jnp.split(modulation, 4)
        tanh_attn = jnp.tanh(gate_attn)
        tanh_ffn = jnp.tanh(gate_ffn)
        text_pack = jnp.concatenate([w_key_text, w_value_text, out_rows], 0)
        text_pack = gather_spread(text_pack).reshape(shards, -1, width)
        key_s = text_pack[:, :text_rows].reshape(-1, width)
        value_s = text_pack[:, text_rows : 2 * text_rows].reshape(-1, width)
        out_s = text_pack[:, 2 * text_rows :].reshape(-1, width)
        gate_in, up_in, down_in, condition = tie(w_gate, w_up, w_down, condition)
        ffn_blocks = jnp.concatenate([line_columns(gate_in), line_columns(up_in)], -1)
        ffn_blocks = lax.all_to_all(ffn_blocks, "ring", split_axis=0, concat_axis=0, tiled=True)
        ffn_s = gather_spread(ffn_blocks.reshape(ring * rows, -1), spread_ffn)
        ffn_s = ffn_s.reshape(shards, pair, ring, rows, -1).transpose(0, 2, 1, 3, 4)
        ffn_s = ffn_s.reshape(width, -1)
        down_s = gather_spread(down_in, spread_ffn)
        ff_own = down_s.shape[0]
        packed = jnp.concatenate(
            [
                modulation,
                condition[0],
                pooled,
                jnp.full((128,), timesteps[0].astype(f32)),
            ]
        )
        clip_facts = lax.all_gather(packed.reshape(-1, 128), "clip", axis=0).reshape(clips, -1)

        normed_all, _ = rms_norm(tokens_all.astype(f32), epsilon)
        gain1 = norm1_gain * (1.0 + scale_attn)
        mix_in = (normed_all * gain1).astype(bf16)
        cot_in, mix_in = tie(cotangent[0], mix_in)
        cot_all = line_gather(cot_in)
        qkv_own = dot(mix_in, qkv_s).reshape(team_rows, 3, heads, head_dim).transpose(1, 2, 0, 3)
        cos_tab, sin_tab = rope_tables(spots, head_dim // 2)
        queries_n, inverse_q = rms_norm(qkv_own[0], head_eps)
        keys_n, inverse_k = rms_norm(qkv_own[1], head_eps)
        queries_b = rotate(queries_n, cos_tab, sin_tab).astype(bf16)
        keys_b = rotate(keys_n, cos_tab, sin_tab).astype(bf16)
        values_b = qkv_own[2].astype(bf16)
        if outer > 1:
            keys_b = lax.all_gather(keys_b, "outer", axis=1, tiled=True)
            values_b = lax.all_gather(values_b, "outer", axis=1, tiled=True)
        scores = ein("hqd,hkd->hqk", queries_b, keys_b) * attn_scale
        top = jnp.max(scores, -1, keepdims=True)
        raised = jnp.exp(scores - top)
        total = jnp.sum(raised, -1, keepdims=True)
        self_out = ein("hqk,hkd->hqd", raised.astype(bf16), values_b) / total
        log_sum = top + jnp.log(total)

        text_part = jnp.stack([dot(cap_part, key_s), dot(cap_part, value_s)]).astype(bf16)
        text_part = text_part.reshape(2, cap_len, inner, own).transpose(2, 1, 0, 3)
        text_own = ring_scatter(slot_blocks(text_part.reshape(inner, cap_len, 2 * own)))
        text_own = text_own.reshape(cap_len, 2, heads, head_dim).transpose(1, 2, 0, 3)
        text_keys_n, inverse_t = rms_norm(text_own[0], head_eps)
        keys_text_b = text_keys_n.astype(bf16)
        values_text_b = text_own[1].astype(bf16)
        cross_scores = ein("hqd,hkd->hqk", queries_b, keys_text_b) * attn_scale
        cross_scores = jnp.where(cap_mask > 0, cross_scores, big_negative)
        cross_probs = jax.nn.softmax(cross_scores, axis=-1)
        cross_probs_b = cross_probs.astype(bf16)
        cross_out = ein("hqk,hkd->hqd", cross_probs_b, values_text_b)
        gate_own = jnp.tanh(lax.dynamic_slice_in_dim(cross_gate, member * heads, heads))
        gate_t = gate_own[:, None, None]
        mixed = self_out + gate_t * cross_out
        mixed_b = mixed.transpose(1, 0, 2).reshape(team_rows, own).astype(bf16)
        attn_out = ring_scatter(row_blocks(dot(mixed_b, out_s).astype(bf16)))

        tokens_f = tokens[0].astype(f32)
        normed1, inverse1 = rms_norm(tokens_f, epsilon)
        resid = tokens_f + tanh_attn * attn_out
        normed2, inverse2 = rms_norm(resid, epsilon)
        gain2 = norm2_gain * (1.0 + scale_ffn)
        ffn_in = line_gather((normed2 * gain2).astype(bf16))
        gate_up = dot(ffn_in, ffn_s)
        gate_pre, up_pre = gate_up[:, :ff_own], gate_up[:, ff_own:]
        sigmoid_g = jax.nn.sigmoid(gate_pre)
        silu_g = gate_pre * sigmoid_g
        hidden_b = (silu_g * up_pre).astype(bf16)
        d_ffn_b = (tanh_ffn * cot_all.astype(f32)).astype(bf16)
        d_hidden = dot_nt(d_ffn_b, down_s)
        silu_slope = sigmoid_g * (1.0 + gate_pre * (1.0 - sigmoid_g))
        d_gate_up = jnp.concatenate(
            [
                (d_hidden * up_pre * silu_slope).astype(bf16),
                (d_hidden * silu_g).astype(bf16),
            ],
            -1,
        )
        d_ffn_in = line_scatter(dot_nt(d_gate_up, ffn_s).astype(bf16))
        d_out = cotangent[0].astype(f32)
        grad_down = dot_tn(hidden_b, d_ffn_b).astype(bf16)
        sum_down = scatter_spread(grad_down, spread_ffn).astype(f32)
        grad_ffn = dot_tn(ffn_in, d_gate_up).astype(bf16)
        grad_ffn = grad_ffn.reshape(shards, ring, pair, rows, -1).transpose(0, 2, 1, 3, 4)
        sum_ffn = scatter_spread(grad_ffn.reshape(width, -1), spread_ffn)
        sum_ffn = sum_ffn.reshape(ring, rows, 2 * ff_own)
        sum_ffn = lax.all_to_all(sum_ffn, "ring", split_axis=0, concat_axis=0, tiled=True)
        sum_gate = back_line_columns(sum_ffn[:, :, :ff_own]).astype(f32)
        sum_up = back_line_columns(sum_ffn[:, :, ff_own:]).astype(f32)

        sum_norm2 = jnp.sum(d_ffn_in * normed2, 0)
        d_resid = d_out + norm_back(normed2, inverse2, d_ffn_in * gain2)
        sum_gate_attn = jnp.sum(d_resid * attn_out, 0)
        d_attn_b = jnp.concatenate(ring_gather((tanh_attn * d_resid).astype(bf16)), 0)
        hidden_b, d_attn_b = tie(hidden_b, d_attn_b)
        ffn_out = line_scatter(dot(hidden_b, down_s).astype(bf16))
        mixed_out = (resid + tanh_ffn * ffn_out).astype(bf16)
        sum_gate_ffn = jnp.sum(d_out * ffn_out, 0)
        grad_out = dot_tn(mixed_b, d_attn_b).astype(bf16)
        sum_out = lax.ppermute(scatter_spread(grad_out), every, from_heads).astype(f32)
        d_mixed = dot_nt(d_attn_b, out_s).reshape(team_rows, heads, head_dim).transpose(1, 0, 2)
        grad_cross = jnp.sum(d_mixed * cross_out, axis=(1, 2)) * (1.0 - gate_own * gate_own)
        d_self_b = d_mixed.astype(bf16)
        d_cross_b = (gate_t * d_mixed).astype(bf16)

        d_cross_probs = ein("hqd,hkd->hqk", d_cross_b, values_text_b)
        d_cross_scores = (
            cross_probs
            * (d_cross_probs - jnp.sum(cross_probs * d_cross_probs, -1, keepdims=True))
        ).astype(bf16)
        d_queries = ein("hqk,hkd->hqd", d_cross_scores, keys_text_b)
        d_text_keys_n = ein("hqk,hqd->hkd", d_cross_scores, queries_b) * attn_scale
        d_text_values = ein("hqk,hqd->hkd", cross_probs_b, d_cross_b)
        if outer > 1:
            d_text_keys_n = lax.psum(d_text_keys_n, "outer")
            d_text_values = lax.psum(d_text_values, "outer")
        d_text_keys = norm_back(text_keys_n, inverse_t, d_text_keys_n)
        text_grads = jnp.stack([d_text_keys, d_text_values]).transpose(2, 0, 1, 3)
        text_grads = text_grads.reshape(cap_len, 2 * own).astype(bf16)
        if outer > 1:
            text_grads = lax.dynamic_slice_in_dim(
                text_grads, lax.axis_index("outer") * inner * cap_rows, inner * cap_rows
            )
        grad_rows = text_grads.shape[0]
        text_grads = in_order(ring_gather(text_grads)).reshape(inner, grad_rows, 2, own)
        text_grads = text_grads.transpose(2, 1, 0, 3).reshape(2, grad_rows, width)
        text_grads = jnp.concatenate([text_grads[0], text_grads[1]], -1)
        sum_text = scatter_spread(dot_tn(cap_own, text_grads).astype(bf16)).astype(f32)
        d_cap = dot_nt(text_grads[:, :width], key_s) + dot_nt(text_grads[:, width:], value_s)

        row_dots = jnp.sum(d_self_b.astype(f32) * self_out, -1, keepdims=True)
        soft_probs = jnp.exp(scores - log_sum)
        d_probs = ein("hqd,hkd->hqk", d_self_b, values_b)
        d_scores_b = (soft_probs * (d_probs - row_dots)).astype(bf16)
        d_queries = (d_queries + ein("hqk,hkd->hqd", d_scores_b, keys_b)) * attn_scale
        d_keys = ein("hqk,hqd->hkd", d_scores_b, queries_b) * attn_scale
        d_values = ein("hqk,hqd->hkd", soft_probs.astype(bf16), d_self_b)
        if outer > 1:
            d_keys = lax.psum_scatter(d_keys, "outer", scatter_dimension=1, tiled=True)
            d_values = lax.psum_scatter(d_values, "outer", scatter_dimension=1, tiled=True)
        d_queries_raw = norm_back(queries_n, inverse_q, rotate(d_queries, cos_tab, -sin_tab))
        d_keys_raw = norm_back(keys_n, inverse_k, rotate(d_keys, cos_tab, -sin_tab))
        d_qkv = jnp.stack([d_queries_raw, d_keys_raw, d_values]).astype(bf16)
        d_qkv = d_qkv.transpose(2, 0, 1, 3).reshape(team_rows, 3 * own)
        d_qkv, sum_ffn, sum_down = tie(d_qkv, sum_ffn, sum_down)
        d_mix_in = ring_scatter(row_blocks(dot_nt(d_qkv, qkv_s).astype(bf16)))
        sum_qkv = scatter_spread(dot_tn(mix_in, d_qkv).astype(bf16))
        sum_qkv = swap_team(sum_qkv.reshape(inner, rows, 3 * own)).reshape(inner, rows, 3, own)
        sum_qkv = sum_qkv.transpose(1, 2, 0, 3).reshape(rows, 3 * width).astype(f32)

        sum_norm1 = jnp.sum(d_mix_in * normed1, 0)
        d_tokens = d_resid + norm_back(normed1, inverse1, d_mix_in * gain1)

        cross_slots = jnp.zeros((128,), f32)
        cross_slots = lax.dynamic_update_slice_in_dim(cross_slots, grad_cross, member * heads, 0)
        early = jnp.concatenate([sum_gate_attn, sum_norm2, sum_gate_ffn, cross_slots])
        early = small_sum(early.reshape(-1, 128))
        late = small_sum(sum_norm1.reshape(-1, 128))
        if outer > 1:
            early = lax.psum(early, "outer")
            late = lax.psum(late, "outer")
        early = lax.all_gather(early, "clip", axis=0).reshape(clips, -1)
        late = lax.all_gather(late, "clip", axis=0).reshape(clips, -1)
        sums = jnp.concatenate([late, early], -1)
        mods = clip_facts[:, :mod_width].reshape(clips, 4, width)
        at = mod_width
        cond_all = clip_facts[:, at : at + cond_width]
        at += cond_width
        pool_all = clip_facts[:, at : at + pooled.shape[0]]
        steps_all = clip_facts[:, at + pooled.shape[0]]
        token_sums = sums[:, :mod_width].reshape(clips, 4, width)
        grad_norm1 = jnp.sum(token_sums[:, 0] * (1.0 + mods[:, 0]), 0)
        grad_norm2 = jnp.sum(token_sums[:, 2] * (1.0 + mods[:, 2]), 0)
        tanh1, tanh3 = jnp.tanh(mods[:, 1]), jnp.tanh(mods[:, 3])
        d_modulation = jnp.concatenate(
            [
                token_sums[:, 0] * norm1_gain,
                token_sums[:, 1] * (1.0 - tanh1 * tanh1),
                token_sums[:, 2] * norm2_gain,
                token_sums[:, 3] * (1.0 - tanh3 * tanh3),
            ],
            -1,
        )
        grad_bias = jnp.sum(d_modulation, 0)
        grad_cross_gate = jnp.sum(sums[:, mod_width : mod_width + head_count], 0)
        row = shard * inner + member
        cond_rows = lax.dynamic_slice_in_dim(
            jax.nn.silu(cond_all).astype(bf16).astype(f32), row * ada_rows, ada_rows, 1
        )
        sum_ada = jnp.sum(cond_rows[:, :, None] * d_modulation[:, None, :], 0)
        d_mod_clip = lax.dynamic_index_in_dim(d_modulation, lax.axis_index("clip"), 0)
        d_cond_own = dot_nt(d_mod_clip.astype(bf16), ada_s)
        d_cond_act = small_gather(d_cond_own.reshape(shards, ada_rows))
        d_cond_act = d_cond_act.transpose(1, 0, 2).reshape(1, cond_width)
        sigmoid_c = jax.nn.sigmoid(condition)
        d_condition = d_cond_act * sigmoid_c * (1.0 + condition * (1.0 - sigmoid_c))
        d_cond_all = lax.all_gather(d_condition[0], "clip", axis=0)
        d_pooled = dot_nt(d_condition.astype(bf16), pool_s).reshape(shards, -1)
        d_pooled = d_pooled[:, :pool_rows].reshape(1, -1)
        first = lax.axis_index("outer") * grad_rows
        own_mask = (first + jnp.arange(grad_rows) < lengths[0]).astype(f32)
        d_cap = (d_cap + own_mask[:, None] * d_pooled / length_f).astype(bf16)
        d_caption = back_columns(swap_team(d_cap.reshape(inner, cap_rows, -1))).astype(f32)
        embed_all = timestep_embed(steps_all, embed_width).astype(bf16).astype(f32)
        embed_rows = lax.dynamic_slice_in_dim(embed_all, row * time_rows, time_rows, 1)
        sum_time = jnp.sum(embed_rows[:, :, None] * d_cond_all[:, None, :], 0)
        pooled_rows = lax.dynamic_slice_in_dim(
            pool_all.astype(bf16).astype(f32), shard * pool_rows, pool_rows, 1
        )
        sum_pool = jnp.sum(pooled_rows[:, :, None] * d_cond_all[:, None, :], 0)
        return (
            mixed_out[None],
            d_tokens[None],
            d_caption[None],
            sum_time,
            sum_pool,
            sum_ada,
            grad_bias,
            grad_norm1,
            sum_qkv,
            sum_text[:, :width],
            sum_text[:, width:],
            grad_cross_gate,
            sum_out,
            grad_norm2,
            sum_gate,
            sum_up,
            sum_down,
        )

    return body


def solution(mesh):
    clips, members = mesh.shape["clip"], mesh.shape["seq"]

    def run(*args):
        inner = math.gcd(args[13].shape[0], members)
        outer, pair = members // inner, math.gcd(inner, 2)
        ring = inner // pair
        names = ("clip", "outer", "ring", "pair")
        fine = Mesh(mesh.devices.reshape(clips, outer, ring, pair), names)
        seq = names[1:]
        every = P(names, None)
        by_token = P("clip", seq, None)
        return jax.shard_map(
            make_body(clips, outer, ring, pair),
            mesh=fine,
            in_specs=(
                by_token,
                by_token,
                P("clip"),
                P("clip"),
                P(None, "clip", seq),
                every,
                every,
                every,
                P(),
                P(),
                every,
                every,
                every,
                P(),
                every,
                P(),
                every,
                every,
                every,
                by_token,
            ),
            out_specs=(
                by_token,
                by_token,
                by_token,
                every,
                every,
                every,
                P(),
                P(),
                every,
                every,
                every,
                P(),
                every,
                P(),
                every,
                every,
                every,
            ),
            check_vma=False,
        )(*args)

    return run
```

```python
import math

import jax
import jax.numpy as jnp
from jax import lax
from jax.sharding import Mesh
from jax.sharding import PartitionSpec as P

epsilon = 1e-05
head_eps = 1e-06
big_negative = -1e30
f32 = jnp.float32
bf16 = jnp.bfloat16


def rope_tables(posint, half_dim):
    pair_ids = jnp.arange(half_dim)
    first_cut = half_dim // 4
    second_cut = first_cut + (half_dim - first_cut) // 2
    group_of = (pair_ids >= first_cut).astype(jnp.int32) + (pair_ids >= second_cut).astype(
        jnp.int32
    )
    starts = jnp.where(group_of == 0, 0, jnp.where(group_of == 1, first_cut, second_cut))
    counts = jnp.where(
        group_of == 0,
        first_cut,
        jnp.where(group_of == 1, second_cut - first_cut, half_dim - second_cut),
    )
    frequency = jnp.exp(
        -math.log(10000.0) * (pair_ids - starts).astype(f32) / counts.astype(f32)
    )
    spots = posint.astype(f32)[:, :, None]
    coords = jnp.where(group_of == 0, spots[0], jnp.where(group_of == 1, spots[1], spots[2]))
    angles = coords * frequency[None, :]
    return (jnp.cos(angles), jnp.sin(angles))


def rotate(vector, cos_tab, sin_tab):
    half_dim = cos_tab.shape[-1]
    front = vector[..., :half_dim]
    behind = vector[..., half_dim:]
    return jnp.concatenate(
        [front * cos_tab - behind * sin_tab, front * sin_tab + behind * cos_tab], -1
    )


def rms_norm(vector, eps_value):
    inverse = lax.rsqrt(jnp.mean(vector * vector, -1, keepdims=True) + eps_value)
    return (vector * inverse, inverse)


def norm_back(normed, inverse, gradient):
    return inverse * (gradient - normed * jnp.mean(gradient * normed, -1, keepdims=True))


def timestep_embed(time_step, embed_width):
    half_dim = embed_width // 2
    frequency = jnp.exp(-math.log(10000.0) * jnp.arange(half_dim, dtype=f32) / half_dim)
    angles = time_step.astype(f32)[..., None] * frequency
    return jnp.concatenate([jnp.cos(angles), jnp.sin(angles)], -1)


def dot(a, b):
    return jnp.dot(a, b, preferred_element_type=f32)


def dot_tn(a, b):
    return lax.dot_general(a, b, (((0,), (0,)), ((), ())), preferred_element_type=f32)


def dot_nt(a, b):
    return lax.dot_general(a, b, (((1,), (1,)), ((), ())), preferred_element_type=f32)


def ein(spec, a, b):
    return jnp.einsum(spec, a, b, preferred_element_type=f32)


def tie(*arrays):
    return lax.optimization_barrier(arrays)


def make_body(clips, outer, ring, pair):
    inner = ring * pair
    shards = clips * outer
    team = ("ring", "pair")
    spread = ("clip", "outer") if outer > 1 else "clip"
    spread_ffn = ("clip", "outer", "pair")
    every = ("clip", "outer", "ring", "pair")
    forward = [(z, (z + 1) % ring) for z in range(ring)]
    crossed = [(x, (x + 1) % pair) for x in range(pair)]
    slots = [(k, e) for k in range(ring) for e in range(pair)]

    def swap_team(x):
        return lax.all_to_all(x, team, split_axis=0, concat_axis=0, tiled=True)

    def gather_spread(x, axes=spread):
        return lax.all_gather(x, axes, axis=0, tiled=True)

    def scatter_spread(x, axes=spread):
        return lax.psum_scatter(x, axes, scatter_dimension=0, tiled=True)

    def ring_gather(x):
        parts, now = [], x
        for k in range(ring):
            parts.append(now)
            other = now
            for _ in range(1, pair):
                other = lax.ppermute(other, "pair", crossed)
                parts.append(other)
            if k + 1 < ring:
                now = lax.ppermute(now, "ring", forward)
        return parts

    def ring_scatter(block_of):
        passed = None
        for step in range(1, ring + 1):
            k = step % ring
            total = block_of(k, 0).astype(f32)
            if pair > 1:
                total = total + lax.ppermute(block_of(k, 1), "pair", crossed).astype(f32)
            if passed is not None:
                total = total + passed.astype(f32)
            if step < ring:
                passed = lax.ppermute(total.astype(bf16), "ring", forward)
        return total

    def row_blocks(x):
        rows = x.shape[0] // inner
        return lambda k, e: x[(k * pair + e) * rows : (k * pair + e + 1) * rows]

    def line_gather(x):
        parts = [x]
        for _ in range(1, ring):
            parts.append(lax.ppermute(parts[-1], "ring", forward))
        return jnp.concatenate(parts, 0)

    def line_scatter(x):
        rows = x.shape[0] // ring
        passed = None
        for step in range(1, ring + 1):
            k = step % ring
            total = x[k * rows : (k + 1) * rows].astype(f32)
            if passed is not None:
                total = total + passed.astype(f32)
            if step < ring:
                passed = lax.ppermute(total.astype(bf16), "ring", forward)
        return total

    def small_sum(x):
        for axis, size in (("pair", pair), ("ring", ring)):
            if size & (size - 1):
                x = lax.psum(x, axis)
                continue
            hop = 1
            while hop < size:
                x = x + lax.ppermute(x, axis, [(i, i ^ hop) for i in range(size)])
                hop *= 2
        return x

    def small_gather(x):
        return swap_team(jnp.broadcast_to(x, (inner,) + x.shape))

    def in_order(parts):
        z, y = lax.axis_index("ring"), lax.axis_index("pair")
        if pair > 1:
            front = [jnp.where(y == 0, parts[2 * k], parts[2 * k + 1]) for k in range(ring)]
            behind = [jnp.where(y == 0, parts[2 * k + 1], parts[2 * k]) for k in range(ring)]
            rows = [jnp.stack([f, g]) for f, g in zip(front, behind)]
        else:
            rows = [part[None] for part in parts]
        twice = jnp.stack((rows[1:] + rows)[::-1])
        whole = lax.dynamic_slice_in_dim(twice, ring - 1 - z, ring)
        return whole.reshape((inner,) + parts[0].shape)

    def slot_blocks(x):
        z, y = lax.axis_index("ring"), lax.axis_index("pair")

        def block_of(k, e):
            spot = lax.rem(z + ring - k, ring) * pair + lax.rem(y + pair - e, pair)
            return lax.dynamic_index_in_dim(x, spot, 0, keepdims=False)

        return block_of

    def by_columns(w):
        rows, columns = w.shape
        blocks = w.reshape(rows, shards, inner, columns // (shards * inner))
        return blocks.transpose(2, 0, 1, 3).reshape(inner, rows, columns // inner)

    def back_columns(w):
        _, rows, columns = w.shape
        blocks = w.reshape(inner, rows, shards, columns // shards)
        return blocks.transpose(1, 2, 0, 3).reshape(rows, inner * columns)

    def line_columns(w):
        rows, columns = w.shape
        blocks = w.reshape(rows, shards, ring, columns // (shards * ring))
        return blocks.transpose(2, 0, 1, 3).reshape(ring, rows, columns // ring)

    def back_line_columns(w):
        _, rows, columns = w.shape
        blocks = w.reshape(ring, rows, shards, columns // shards)
        return blocks.transpose(1, 2, 0, 3).reshape(rows, ring * columns)

    def body(
        tokens,
        caption,
        lengths,
        timesteps,
        positions,
        w_time,
        w_pool,
        w_ada,
        b_ada,
        norm1_gain,
        w_qkv,
        w_key_text,
        w_value_text,
        cross_gate,
        w_out,
        norm2_gain,
        w_gate,
        w_up,
        w_down,
        cotangent,
    ):
        head_count = cross_gate.shape[0]
        width = tokens.shape[2]
        head_dim = width // head_count
        heads = head_count // inner
        own = heads * head_dim
        tok_rows = tokens.shape[1]
        team_rows = tok_rows * inner
        cap_rows = caption.shape[1]
        cond_width = w_pool.shape[1]
        mod_width = b_ada.shape[0]
        attn_scale = 1.0 / math.sqrt(head_dim)
        member = lax.axis_index(team)
        shard = lax.axis_index(spread)
        length_f = lengths[0].astype(f32)

        cap_blocks = by_columns(caption[0])
        cap_part = swap_team(cap_blocks).reshape(inner * cap_rows, -1)
        cap_own = cap_part
        if outer > 1:
            cap_part = lax.all_gather(cap_part, "outer", axis=0, tiled=True)
        cap_len = cap_part.shape[0]
        pool_rows, time_rows, ada_rows = w_pool.shape[0], w_time.shape[0], w_ada.shape[0]
        pool_s = gather_spread(jnp.concatenate([w_pool, w_time], 0))
        ada_s = gather_spread(w_ada)
        rows = w_qkv.shape[0]
        qkv_blocks = w_qkv.reshape(rows, 3, inner, own).transpose(2, 0, 1, 3)
        qkv_blocks = qkv_blocks.reshape(inner, rows, 3 * own)
        qkv_s = gather_spread(swap_team(qkv_blocks).reshape(inner * rows, 3 * own))
        spots = positions[:, 0, :].astype(bf16).T
        spots = jnp.concatenate([spots, jnp.zeros((tok_rows, 125), bf16)], -1)
        tokens_all = jnp.concatenate(
            ring_gather(jnp.concatenate([tokens[0], spots], -1)), 0
        )
        spots = tokens_all[:, width : width + 3].astype(f32).T
        tokens_all = tokens_all[:, :width]
        to_heads = [
            (r, (r % shards) * inner + r // shards) for r in range(shards * inner)
        ]
        from_heads = [(b, a) for a, b in to_heads]
        out_rows = lax.ppermute(w_out, every, to_heads)
        text_rows = w_key_text.shape[0]

        cap_mask = (jnp.arange(cap_len) < lengths[0]).astype(f32)
        pooled = jnp.sum(cap_part.astype(f32) * cap_mask[:, None], 0) / length_f
        pooled_b = pooled.astype(bf16)
        embed_width = time_rows * shards * inner
        time_embed = timestep_embed(timesteps[0], embed_width).astype(bf16)
        time_own = lax.dynamic_index_in_dim(
            time_embed.reshape(shards, inner, time_rows), member, 1, keepdims=False
        )
        facts = jnp.concatenate([pooled_b.reshape(shards, pool_rows), time_own], 1)
        condition = small_sum(dot(facts.reshape(1, -1), pool_s))
        cond_b = jax.nn.silu(condition).astype(bf16)
        cond_own = lax.dynamic_index_in_dim(
            cond_b.reshape(shards, inner, ada_rows), member, 1, keepdims=False
        ).reshape(1, -1)
        modulation = small_sum(dot(cond_own, ada_s)).reshape(-1) + b_ada
        scale_attn, gate_attn, scale_ffn, gate_ffn = jnp.split(modulation, 4)
        tanh_attn = jnp.tanh(gate_attn)
        tanh_ffn = jnp.tanh(gate_ffn)
        text_pack = jnp.concatenate([w_key_text, w_value_text, out_rows], 0)
        text_pack = gather_spread(text_pack).reshape(shards, -1, width)
        key_s = text_pack[:, :text_rows].reshape(-1, width)
        value_s = text_pack[:, text_rows : 2 * text_rows].reshape(-1, width)
        out_s = text_pack[:, 2 * text_rows :].reshape(-1, width)
        gate_in, up_in, down_in, condition = tie(w_gate, w_up, w_down, condition)
        ffn_blocks = jnp.concatenate([line_columns(gate_in), line_columns(up_in)], -1)
        ffn_blocks = lax.all_to_all(ffn_blocks, "ring", split_axis=0, concat_axis=0, tiled=True)
        ffn_s = gather_spread(ffn_blocks.reshape(ring * rows, -1), spread_ffn)
        ffn_s = ffn_s.reshape(shards, pair, ring, rows, -1).transpose(0, 2, 1, 3, 4)
        ffn_s = ffn_s.reshape(width, -1)
        down_s = gather_spread(down_in, spread_ffn)
        ff_own = down_s.shape[0]
        packed = jnp.concatenate(
            [
                modulation,
                condition[0],
                pooled,
                jnp.full((128,), timesteps[0].astype(f32)),
            ]
        )

        normed_all, _ = rms_norm(tokens_all.astype(f32), epsilon)
        gain1 = norm1_gain * (1.0 + scale_attn)
        mix_in = (normed_all * gain1).astype(bf16)
        cot_in, mix_in = tie(cotangent[0], mix_in)
        cot_all = line_gather(cot_in)
        qkv_own = dot(mix_in, qkv_s).reshape(team_rows, 3, heads, head_dim).transpose(1, 2, 0, 3)
        cos_tab, sin_tab = rope_tables(spots, head_dim // 2)
        queries_n, inverse_q = rms_norm(qkv_own[0], head_eps)
        keys_n, inverse_k = rms_norm(qkv_own[1], head_eps)
        queries_b = rotate(queries_n, cos_tab, sin_tab).astype(bf16)
        keys_b = rotate(keys_n, cos_tab, sin_tab).astype(bf16)
        values_b = qkv_own[2].astype(bf16)
        if outer > 1:
            keys_b = lax.all_gather(keys_b, "outer", axis=1, tiled=True)
            values_b = lax.all_gather(values_b, "outer", axis=1, tiled=True)
        scores = ein("hqd,hkd->hqk", queries_b, keys_b) * attn_scale
        top = jnp.max(scores, -1, keepdims=True)
        raised = jnp.exp(scores - top)
        total = jnp.sum(raised, -1, keepdims=True)
        self_out = ein("hqk,hkd->hqd", raised.astype(bf16), values_b) / total
        log_sum = top + jnp.log(total)

        text_part = jnp.stack([dot(cap_part, key_s), dot(cap_part, value_s)]).astype(bf16)
        text_part = text_part.reshape(2, cap_len, inner, own).transpose(2, 1, 0, 3)
        text_own = swap_team(text_part.reshape(inner, cap_len, 2 * own))
        text_own = jnp.sum(text_own.astype(f32), 0)
        text_own = text_own.reshape(cap_len, 2, heads, head_dim).transpose(1, 2, 0, 3)
        text_keys_n, inverse_t = rms_norm(text_own[0], head_eps)
        keys_text_b = text_keys_n.astype(bf16)
        values_text_b = text_own[1].astype(bf16)
        cross_scores = ein("hqd,hkd->hqk", queries_b, keys_text_b) * attn_scale
        cross_scores = jnp.where(cap_mask > 0, cross_scores, big_negative)
        cross_probs = jax.nn.softmax(cross_scores, axis=-1)
        cross_probs_b = cross_probs.astype(bf16)
        cross_out = ein("hqk,hkd->hqd", cross_probs_b, values_text_b)
        gate_own = jnp.tanh(lax.dynamic_slice_in_dim(cross_gate, member * heads, heads))
        gate_t = gate_own[:, None, None]
        mixed = self_out + gate_t * cross_out
        mixed_b = mixed.transpose(1, 0, 2).reshape(team_rows, own).astype(bf16)
        attn_out = ring_scatter(row_blocks(dot(mixed_b, out_s).astype(bf16)))

        tokens_f = tokens[0].astype(f32)
        normed1, inverse1 = rms_norm(tokens_f, epsilon)
        resid = tokens_f + tanh_attn * attn_out
        normed2, inverse2 = rms_norm(resid, epsilon)
        gain2 = norm2_gain * (1.0 + scale_ffn)
        ffn_in = line_gather((normed2 * gain2).astype(bf16))
        gate_up = dot(ffn_in, ffn_s)
        gate_pre, up_pre = gate_up[:, :ff_own], gate_up[:, ff_own:]
        sigmoid_g = jax.nn.sigmoid(gate_pre)
        silu_g = gate_pre * sigmoid_g
        hidden_b = (silu_g * up_pre).astype(bf16)
        d_ffn_b = (tanh_ffn * cot_all.astype(f32)).astype(bf16)
        d_hidden = dot_nt(d_ffn_b, down_s)
        silu_slope = sigmoid_g * (1.0 + gate_pre * (1.0 - sigmoid_g))
        d_gate_up = jnp.concatenate(
            [
                (d_hidden * up_pre * silu_slope).astype(bf16),
                (d_hidden * silu_g).astype(bf16),
            ],
            -1,
        )
        d_ffn_in = line_scatter(dot_nt(d_gate_up, ffn_s).astype(bf16))
        d_out = cotangent[0].astype(f32)
        grad_down = dot_tn(hidden_b, d_ffn_b).astype(bf16)
        sum_down = scatter_spread(grad_down, spread_ffn).astype(f32)
        grad_ffn = dot_tn(ffn_in, d_gate_up).astype(bf16)
        grad_ffn = grad_ffn.reshape(shards, ring, pair, rows, -1).transpose(0, 2, 1, 3, 4)
        sum_ffn = scatter_spread(grad_ffn.reshape(width, -1), spread_ffn)
        sum_ffn = sum_ffn.reshape(ring, rows, 2 * ff_own)
        sum_ffn = lax.all_to_all(sum_ffn, "ring", split_axis=0, concat_axis=0, tiled=True)
        sum_gate = back_line_columns(sum_ffn[:, :, :ff_own]).astype(f32)
        sum_up = back_line_columns(sum_ffn[:, :, ff_own:]).astype(f32)

        sum_norm2 = jnp.sum(d_ffn_in * normed2, 0)
        d_resid = d_out + norm_back(normed2, inverse2, d_ffn_in * gain2)
        sum_gate_attn = jnp.sum(d_resid * attn_out, 0)
        d_attn_b = jnp.concatenate(ring_gather((tanh_attn * d_resid).astype(bf16)), 0)
        hidden_b, d_attn_b = tie(hidden_b, d_attn_b)
        ffn_out = line_scatter(dot(hidden_b, down_s).astype(bf16))
        mixed_out = (resid + tanh_ffn * ffn_out).astype(bf16)
        sum_gate_ffn = jnp.sum(d_out * ffn_out, 0)
        grad_out = dot_tn(mixed_b, d_attn_b).astype(bf16)
        sum_out = lax.ppermute(scatter_spread(grad_out), every, from_heads).astype(f32)
        d_mixed = dot_nt(d_attn_b, out_s).reshape(team_rows, heads, head_dim).transpose(1, 0, 2)
        grad_cross = jnp.sum(d_mixed * cross_out, axis=(1, 2)) * (1.0 - gate_own * gate_own)
        d_self_b = d_mixed.astype(bf16)
        d_cross_b = (gate_t * d_mixed).astype(bf16)

        d_cross_probs = ein("hqd,hkd->hqk", d_cross_b, values_text_b)
        d_cross_scores = (
            cross_probs
            * (d_cross_probs - jnp.sum(cross_probs * d_cross_probs, -1, keepdims=True))
        ).astype(bf16)
        d_queries = ein("hqk,hkd->hqd", d_cross_scores, keys_text_b)
        d_text_keys_n = ein("hqk,hqd->hkd", d_cross_scores, queries_b) * attn_scale
        d_text_values = ein("hqk,hqd->hkd", cross_probs_b, d_cross_b)
        if outer > 1:
            d_text_keys_n = lax.psum(d_text_keys_n, "outer")
            d_text_values = lax.psum(d_text_values, "outer")
        d_text_keys = norm_back(text_keys_n, inverse_t, d_text_keys_n)
        text_grads = jnp.stack([d_text_keys, d_text_values]).transpose(2, 0, 1, 3)
        text_grads = text_grads.reshape(cap_len, 2 * own).astype(bf16)
        if outer > 1:
            text_grads = lax.dynamic_slice_in_dim(
                text_grads, lax.axis_index("outer") * inner * cap_rows, inner * cap_rows
            )
        grad_rows = text_grads.shape[0]
        text_grads = small_gather(text_grads).reshape(inner, grad_rows, 2, own)
        text_grads = text_grads.transpose(2, 1, 0, 3).reshape(2, grad_rows, width)
        text_grads = jnp.concatenate([text_grads[0], text_grads[1]], -1)
        sum_text = scatter_spread(dot_tn(cap_own, text_grads).astype(bf16)).astype(f32)
        d_cap = dot_nt(text_grads[:, :width], key_s) + dot_nt(text_grads[:, width:], value_s)

        row_dots = jnp.sum(d_self_b.astype(f32) * self_out, -1, keepdims=True)
        soft_probs = jnp.exp(scores - log_sum)
        d_probs = ein("hqd,hkd->hqk", d_self_b, values_b)
        d_scores_b = (soft_probs * (d_probs - row_dots)).astype(bf16)
        d_queries = (d_queries + ein("hqk,hkd->hqd", d_scores_b, keys_b)) * attn_scale
        d_keys = ein("hqk,hqd->hkd", d_scores_b, queries_b) * attn_scale
        d_values = ein("hqk,hqd->hkd", soft_probs.astype(bf16), d_self_b)
        if outer > 1:
            d_keys = lax.psum_scatter(d_keys, "outer", scatter_dimension=1, tiled=True)
            d_values = lax.psum_scatter(d_values, "outer", scatter_dimension=1, tiled=True)
        d_queries_raw = norm_back(queries_n, inverse_q, rotate(d_queries, cos_tab, -sin_tab))
        d_keys_raw = norm_back(keys_n, inverse_k, rotate(d_keys, cos_tab, -sin_tab))
        d_qkv = jnp.stack([d_queries_raw, d_keys_raw, d_values]).astype(bf16)
        d_qkv = d_qkv.transpose(2, 0, 1, 3).reshape(team_rows, 3 * own)
        d_qkv, sum_ffn, sum_down = tie(d_qkv, sum_ffn, sum_down)
        d_mix_in = ring_scatter(row_blocks(dot_nt(d_qkv, qkv_s).astype(bf16)))
        sum_qkv = scatter_spread(dot_tn(mix_in, d_qkv).astype(bf16))
        sum_qkv = swap_team(sum_qkv.reshape(inner, rows, 3 * own)).reshape(inner, rows, 3, own)
        sum_qkv = sum_qkv.transpose(1, 2, 0, 3).reshape(rows, 3 * width).astype(f32)

        sum_norm1 = jnp.sum(d_mix_in * normed1, 0)
        d_tokens = d_resid + norm_back(normed1, inverse1, d_mix_in * gain1)

        cross_slots = jnp.zeros((128,), f32)
        cross_slots = lax.dynamic_update_slice_in_dim(cross_slots, grad_cross, member * heads, 0)
        early = jnp.concatenate([sum_gate_attn, sum_norm2, sum_gate_ffn, cross_slots])
        early = small_sum(early.reshape(-1, 128))
        late = small_sum(sum_norm1.reshape(-1, 128))
        if outer > 1:
            early = lax.psum(early, "outer")
            late = lax.psum(late, "outer")
        clip_sums = jnp.concatenate([late, early], 0)
        clip_facts = jnp.concatenate([clip_sums, packed.reshape(-1, 128)], 0)
        clip_facts = lax.all_gather(clip_facts, "clip", axis=0).reshape(clips, -1)
        sums = clip_facts[:, : clip_sums.size]
        clip_facts = clip_facts[:, clip_sums.size :]
        mods = clip_facts[:, :mod_width].reshape(clips, 4, width)
        at = mod_width
        cond_all = clip_facts[:, at : at + cond_width]
        at += cond_width
        pool_all = clip_facts[:, at : at + pooled.shape[0]]
        steps_all = clip_facts[:, at + pooled.shape[0]]
        token_sums = sums[:, :mod_width].reshape(clips, 4, width)
        grad_norm1 = jnp.sum(token_sums[:, 0] * (1.0 + mods[:, 0]), 0)
        grad_norm2 = jnp.sum(token_sums[:, 2] * (1.0 + mods[:, 2]), 0)
        tanh1, tanh3 = jnp.tanh(mods[:, 1]), jnp.tanh(mods[:, 3])
        d_modulation = jnp.concatenate(
            [
                token_sums[:, 0] * norm1_gain,
                token_sums[:, 1] * (1.0 - tanh1 * tanh1),
                token_sums[:, 2] * norm2_gain,
                token_sums[:, 3] * (1.0 - tanh3 * tanh3),
            ],
            -1,
        )
        grad_bias = jnp.sum(d_modulation, 0)
        grad_cross_gate = jnp.sum(sums[:, mod_width : mod_width + head_count], 0)
        row = shard * inner + member
        cond_rows = lax.dynamic_slice_in_dim(
            jax.nn.silu(cond_all).astype(bf16).astype(f32), row * ada_rows, ada_rows, 1
        )
        sum_ada = jnp.sum(cond_rows[:, :, None] * d_modulation[:, None, :], 0)
        d_mod_clip = lax.dynamic_index_in_dim(d_modulation, lax.axis_index("clip"), 0)
        d_cond_own = dot_nt(d_mod_clip.astype(bf16), ada_s)
        d_cond_act = small_gather(d_cond_own.reshape(shards, ada_rows))
        d_cond_act = d_cond_act.transpose(1, 0, 2).reshape(1, cond_width)
        sigmoid_c = jax.nn.sigmoid(condition)
        d_condition = d_cond_act * sigmoid_c * (1.0 + condition * (1.0 - sigmoid_c))
        d_cond_all = lax.all_gather(d_condition[0], "clip", axis=0)
        d_pooled = dot_nt(d_condition.astype(bf16), pool_s).reshape(shards, -1)
        d_pooled = d_pooled[:, :pool_rows].reshape(1, -1)
        first = lax.axis_index("outer") * grad_rows
        own_mask = (first + jnp.arange(grad_rows) < lengths[0]).astype(f32)
        d_cap = (d_cap + own_mask[:, None] * d_pooled / length_f).astype(bf16)
        d_caption = back_columns(swap_team(d_cap.reshape(inner, cap_rows, -1))).astype(f32)
        embed_all = timestep_embed(steps_all, embed_width).astype(bf16).astype(f32)
        embed_rows = lax.dynamic_slice_in_dim(embed_all, row * time_rows, time_rows, 1)
        sum_time = jnp.sum(embed_rows[:, :, None] * d_cond_all[:, None, :], 0)
        pooled_rows = lax.dynamic_slice_in_dim(
            pool_all.astype(bf16).astype(f32), shard * pool_rows, pool_rows, 1
        )
        sum_pool = jnp.sum(pooled_rows[:, :, None] * d_cond_all[:, None, :], 0)
        return (
            mixed_out[None],
            d_tokens[None],
            d_caption[None],
            sum_time,
            sum_pool,
            sum_ada,
            grad_bias,
            grad_norm1,
            sum_qkv,
            sum_text[:, :width],
            sum_text[:, width:],
            grad_cross_gate,
            sum_out,
            grad_norm2,
            sum_gate,
            sum_up,
            sum_down,
        )

    return body


def solution(mesh):
    clips, members = mesh.shape["clip"], mesh.shape["seq"]

    def run(*args):
        inner = math.gcd(args[13].shape[0], members)
        outer, pair = members // inner, math.gcd(inner, 2)
        ring = inner // pair
        names = ("clip", "outer", "ring", "pair")
        fine = Mesh(mesh.devices.reshape(clips, outer, ring, pair), names)
        seq = names[1:]
        every = P(names, None)
        by_token = P("clip", seq, None)
        return jax.shard_map(
            make_body(clips, outer, ring, pair),
            mesh=fine,
            in_specs=(
                by_token,
                by_token,
                P("clip"),
                P("clip"),
                P(None, "clip", seq),
                every,
                every,
                every,
                P(),
                P(),
                every,
                every,
                every,
                P(),
                every,
                P(),
                every,
                every,
                every,
                by_token,
            ),
            out_specs=(
                by_token,
                by_token,
                by_token,
                every,
                every,
                every,
                P(),
                P(),
                every,
                every,
                every,
                P(),
                every,
                P(),
                every,
                every,
                every,
            ),
            check_vma=False,
        )(*args)

    return run
```

```python
import math

import jax
import jax.numpy as jnp
from jax import lax
from jax.sharding import Mesh
from jax.sharding import PartitionSpec as P

epsilon = 1e-05
head_eps = 1e-06
big_negative = -1e30
f32 = jnp.float32
bf16 = jnp.bfloat16


def rope_tables(posint, half_dim):
    pair_ids = jnp.arange(half_dim)
    first_cut = half_dim // 4
    second_cut = first_cut + (half_dim - first_cut) // 2
    group_of = (pair_ids >= first_cut).astype(jnp.int32) + (pair_ids >= second_cut).astype(
        jnp.int32
    )
    starts = jnp.where(group_of == 0, 0, jnp.where(group_of == 1, first_cut, second_cut))
    counts = jnp.where(
        group_of == 0,
        first_cut,
        jnp.where(group_of == 1, second_cut - first_cut, half_dim - second_cut),
    )
    frequency = jnp.exp(
        -math.log(10000.0) * (pair_ids - starts).astype(f32) / counts.astype(f32)
    )
    spots = posint.astype(f32)[:, :, None]
    coords = jnp.where(group_of == 0, spots[0], jnp.where(group_of == 1, spots[1], spots[2]))
    angles = coords * frequency[None, :]
    return (jnp.cos(angles), jnp.sin(angles))


def rotate(vector, cos_tab, sin_tab):
    half_dim = cos_tab.shape[-1]
    front = vector[..., :half_dim]
    behind = vector[..., half_dim:]
    return jnp.concatenate(
        [front * cos_tab - behind * sin_tab, front * sin_tab + behind * cos_tab], -1
    )


def rms_norm(vector, eps_value):
    inverse = lax.rsqrt(jnp.mean(vector * vector, -1, keepdims=True) + eps_value)
    return (vector * inverse, inverse)


def norm_back(normed, inverse, gradient):
    return inverse * (gradient - normed * jnp.mean(gradient * normed, -1, keepdims=True))


def timestep_embed(time_step, embed_width):
    half_dim = embed_width // 2
    frequency = jnp.exp(-math.log(10000.0) * jnp.arange(half_dim, dtype=f32) / half_dim)
    angles = time_step.astype(f32)[..., None] * frequency
    return jnp.concatenate([jnp.cos(angles), jnp.sin(angles)], -1)


def dot(a, b):
    return jnp.dot(a, b, preferred_element_type=f32)


def dot_tn(a, b):
    return lax.dot_general(a, b, (((0,), (0,)), ((), ())), preferred_element_type=f32)


def dot_nt(a, b):
    return lax.dot_general(a, b, (((1,), (1,)), ((), ())), preferred_element_type=f32)


def ein(spec, a, b):
    return jnp.einsum(spec, a, b, preferred_element_type=f32)


def tie(*arrays):
    return lax.optimization_barrier(arrays)


def make_body(clips, outer, ring, pair):
    inner = ring * pair
    shards = clips * outer
    team = ("ring", "pair")
    spread = ("clip", "outer") if outer > 1 else "clip"
    spread_ffn = ("clip", "outer", "pair")
    every = ("clip", "outer", "ring", "pair")
    forward = [(z, (z + 1) % ring) for z in range(ring)]
    crossed = [(x, (x + 1) % pair) for x in range(pair)]
    slots = [(k, e) for k in range(ring) for e in range(pair)]

    def swap_team(x):
        return lax.all_to_all(x, team, split_axis=0, concat_axis=0, tiled=True)

    def gather_spread(x, axes=spread):
        return lax.all_gather(x, axes, axis=0, tiled=True)

    def scatter_spread(x, axes=spread):
        return lax.psum_scatter(x, axes, scatter_dimension=0, tiled=True)

    def ring_gather(x):
        parts, now = [], x
        for k in range(ring):
            parts.append(now)
            other = now
            for _ in range(1, pair):
                other = lax.ppermute(other, "pair", crossed)
                parts.append(other)
            if k + 1 < ring:
                now = lax.ppermute(now, "ring", forward)
        return parts

    def ring_scatter(block_of):
        passed = None
        for step in range(1, ring + 1):
            k = step % ring
            total = block_of(k, 0).astype(f32)
            if pair > 1:
                total = total + lax.ppermute(block_of(k, 1), "pair", crossed).astype(f32)
            if passed is not None:
                total = total + passed.astype(f32)
            if step < ring:
                passed = lax.ppermute(total.astype(bf16), "ring", forward)
        return total

    def row_blocks(x):
        rows = x.shape[0] // inner
        return lambda k, e: x[(k * pair + e) * rows : (k * pair + e + 1) * rows]

    def line_gather(x):
        parts = [x]
        for _ in range(1, ring):
            parts.append(lax.ppermute(parts[-1], "ring", forward))
        return jnp.concatenate(parts, 0)

    def line_scatter(x):
        rows = x.shape[0] // ring
        passed = None
        for step in range(1, ring + 1):
            k = step % ring
            total = x[k * rows : (k + 1) * rows].astype(f32)
            if passed is not None:
                total = total + passed.astype(f32)
            if step < ring:
                passed = lax.ppermute(total.astype(bf16), "ring", forward)
        return total

    def small_sum(x):
        for axis, size in (("pair", pair), ("ring", ring)):
            if size & (size - 1):
                x = lax.psum(x, axis)
                continue
            hop = 1
            while hop < size:
                x = x + lax.ppermute(x, axis, [(i, i ^ hop) for i in range(size)])
                hop *= 2
        return x

    def small_gather(x):
        return swap_team(jnp.broadcast_to(x, (inner,) + x.shape))

    def in_order(parts):
        z, y = lax.axis_index("ring"), lax.axis_index("pair")
        if pair > 1:
            front = [jnp.where(y == 0, parts[2 * k], parts[2 * k + 1]) for k in range(ring)]
            behind = [jnp.where(y == 0, parts[2 * k + 1], parts[2 * k]) for k in range(ring)]
            rows = [jnp.stack([f, g]) for f, g in zip(front, behind)]
        else:
            rows = [part[None] for part in parts]
        twice = jnp.stack((rows[1:] + rows)[::-1])
        whole = lax.dynamic_slice_in_dim(twice, ring - 1 - z, ring)
        return whole.reshape((inner,) + parts[0].shape)

    def slot_blocks(x):
        z, y = lax.axis_index("ring"), lax.axis_index("pair")

        def block_of(k, e):
            spot = lax.rem(z + ring - k, ring) * pair + lax.rem(y + pair - e, pair)
            return lax.dynamic_index_in_dim(x, spot, 0, keepdims=False)

        return block_of

    def by_columns(w):
        rows, columns = w.shape
        blocks = w.reshape(rows, shards, inner, columns // (shards * inner))
        return blocks.transpose(2, 0, 1, 3).reshape(inner, rows, columns // inner)

    def back_columns(w):
        _, rows, columns = w.shape
        blocks = w.reshape(inner, rows, shards, columns // shards)
        return blocks.transpose(1, 2, 0, 3).reshape(rows, inner * columns)

    def line_columns(w):
        rows, columns = w.shape
        blocks = w.reshape(rows, shards, ring, columns // (shards * ring))
        return blocks.transpose(2, 0, 1, 3).reshape(ring, rows, columns // ring)

    def back_line_columns(w):
        _, rows, columns = w.shape
        blocks = w.reshape(ring, rows, shards, columns // shards)
        return blocks.transpose(1, 2, 0, 3).reshape(rows, ring * columns)

    def body(
        tokens,
        caption,
        lengths,
        timesteps,
        positions,
        w_time,
        w_pool,
        w_ada,
        b_ada,
        norm1_gain,
        w_qkv,
        w_key_text,
        w_value_text,
        cross_gate,
        w_out,
        norm2_gain,
        w_gate,
        w_up,
        w_down,
        cotangent,
    ):
        head_count = cross_gate.shape[0]
        width = tokens.shape[2]
        head_dim = width // head_count
        heads = head_count // inner
        own = heads * head_dim
        tok_rows = tokens.shape[1]
        team_rows = tok_rows * inner
        cap_rows = caption.shape[1]
        cond_width = w_pool.shape[1]
        mod_width = b_ada.shape[0]
        attn_scale = 1.0 / math.sqrt(head_dim)
        member = lax.axis_index(team)
        shard = lax.axis_index(spread)
        length_f = lengths[0].astype(f32)

        cap_blocks = by_columns(caption[0])
        cap_part = swap_team(cap_blocks).reshape(inner * cap_rows, -1)
        cap_own = cap_part
        if outer > 1:
            cap_part = lax.all_gather(cap_part, "outer", axis=0, tiled=True)
        cap_len = cap_part.shape[0]
        pool_rows, time_rows, ada_rows = w_pool.shape[0], w_time.shape[0], w_ada.shape[0]
        pool_s = gather_spread(jnp.concatenate([w_pool, w_time], 0))
        ada_s = gather_spread(w_ada)
        rows = w_qkv.shape[0]
        qkv_blocks = w_qkv.reshape(rows, 3, inner, own).transpose(2, 0, 1, 3)
        qkv_blocks = qkv_blocks.reshape(inner, rows, 3 * own)
        qkv_s = gather_spread(swap_team(qkv_blocks).reshape(inner * rows, 3 * own))
        spots = positions[:, 0, :].astype(bf16).T
        spots = jnp.concatenate([spots, jnp.zeros((tok_rows, 125), bf16)], -1)
        tokens_all = jnp.concatenate(
            ring_gather(jnp.concatenate([tokens[0], spots], -1)), 0
        )
        spots = tokens_all[:, width : width + 3].astype(f32).T
        tokens_all = tokens_all[:, :width]
        to_heads = [
            (r, (r % shards) * inner + r // shards) for r in range(shards * inner)
        ]
        from_heads = [(b, a) for a, b in to_heads]
        out_rows = lax.ppermute(w_out, every, to_heads)
        text_rows = w_key_text.shape[0]

        cap_mask = (jnp.arange(cap_len) < lengths[0]).astype(f32)
        pooled = jnp.sum(cap_part.astype(f32) * cap_mask[:, None], 0) / length_f
        pooled_b = pooled.astype(bf16)
        embed_width = time_rows * shards * inner
        time_embed = timestep_embed(timesteps[0], embed_width).astype(bf16)
        time_own = lax.dynamic_index_in_dim(
            time_embed.reshape(shards, inner, time_rows), member, 1, keepdims=False
        )
        facts = jnp.concatenate([pooled_b.reshape(shards, pool_rows), time_own], 1)
        condition = small_sum(dot(facts.reshape(1, -1), pool_s))
        cond_b = jax.nn.silu(condition).astype(bf16)
        cond_own = lax.dynamic_index_in_dim(
            cond_b.reshape(shards, inner, ada_rows), member, 1, keepdims=False
        ).reshape(1, -1)
        modulation = small_sum(dot(cond_own, ada_s)).reshape(-1) + b_ada
        scale_attn, gate_attn, scale_ffn, gate_ffn = jnp.split(modulation, 4)
        tanh_attn = jnp.tanh(gate_attn)
        tanh_ffn = jnp.tanh(gate_ffn)
        text_pack = jnp.concatenate([w_key_text, w_value_text, out_rows], 0)
        text_pack = gather_spread(text_pack).reshape(shards, -1, width)
        key_s = text_pack[:, :text_rows].reshape(-1, width)
        value_s = text_pack[:, text_rows : 2 * text_rows].reshape(-1, width)
        out_s = text_pack[:, 2 * text_rows :].reshape(-1, width)
        gate_in, up_in, down_in, condition = tie(w_gate, w_up, w_down, condition)
        ffn_blocks = jnp.concatenate([line_columns(gate_in), line_columns(up_in)], -1)
        ffn_blocks = lax.all_to_all(ffn_blocks, "ring", split_axis=0, concat_axis=0, tiled=True)
        ffn_s = gather_spread(ffn_blocks.reshape(ring * rows, -1), spread_ffn)
        ffn_s = ffn_s.reshape(shards, pair, ring, rows, -1).transpose(0, 2, 1, 3, 4)
        ffn_s = ffn_s.reshape(width, -1)
        down_s = gather_spread(down_in, spread_ffn)
        ff_own = down_s.shape[0]
        packed = jnp.concatenate(
            [
                modulation,
                condition[0],
                pooled,
                jnp.full((128,), timesteps[0].astype(f32)),
            ]
        )

        normed_all, _ = rms_norm(tokens_all.astype(f32), epsilon)
        gain1 = norm1_gain * (1.0 + scale_attn)
        mix_in = (normed_all * gain1).astype(bf16)
        cot_in, mix_in = tie(cotangent[0], mix_in)
        cot_all = line_gather(cot_in)
        qkv_own = dot(mix_in, qkv_s).reshape(team_rows, 3, heads, head_dim).transpose(1, 2, 0, 3)
        cos_tab, sin_tab = rope_tables(spots, head_dim // 2)
        queries_n, inverse_q = rms_norm(qkv_own[0], head_eps)
        keys_n, inverse_k = rms_norm(qkv_own[1], head_eps)
        queries_b = rotate(queries_n, cos_tab, sin_tab).astype(bf16)
        keys_b = rotate(keys_n, cos_tab, sin_tab).astype(bf16)
        values_b = qkv_own[2].astype(bf16)
        if outer > 1:
            keys_b = lax.all_gather(keys_b, "outer", axis=1, tiled=True)
            values_b = lax.all_gather(values_b, "outer", axis=1, tiled=True)
        scores = ein("hqd,hkd->hqk", queries_b, keys_b) * attn_scale
        top = jnp.max(scores, -1, keepdims=True)
        raised = jnp.exp(scores - top)
        total = jnp.sum(raised, -1, keepdims=True)
        self_out = ein("hqk,hkd->hqd", raised.astype(bf16), values_b) / total
        log_sum = top + jnp.log(total)

        text_part = jnp.stack([dot(cap_part, key_s), dot(cap_part, value_s)]).astype(bf16)
        text_part = text_part.reshape(2, cap_len, inner, own).transpose(2, 1, 0, 3)
        text_own = swap_team(text_part.reshape(inner, cap_len, 2 * own))
        text_own = jnp.sum(text_own.astype(f32), 0)
        text_own = text_own.reshape(cap_len, 2, heads, head_dim).transpose(1, 2, 0, 3)
        text_keys_n, inverse_t = rms_norm(text_own[0], head_eps)
        keys_text_b = text_keys_n.astype(bf16)
        values_text_b = text_own[1].astype(bf16)
        cross_scores = ein("hqd,hkd->hqk", queries_b, keys_text_b) * attn_scale
        cross_scores = jnp.where(cap_mask > 0, cross_scores, big_negative)
        cross_probs = jax.nn.softmax(cross_scores, axis=-1)
        cross_probs_b = cross_probs.astype(bf16)
        cross_out = ein("hqk,hkd->hqd", cross_probs_b, values_text_b)
        gate_own = jnp.tanh(lax.dynamic_slice_in_dim(cross_gate, member * heads, heads))
        gate_t = gate_own[:, None, None]
        mixed = self_out + gate_t * cross_out
        mixed_b = mixed.transpose(1, 0, 2).reshape(team_rows, own).astype(bf16)
        attn_out = ring_scatter(row_blocks(dot(mixed_b, out_s).astype(bf16)))

        tokens_f = tokens[0].astype(f32)
        normed1, inverse1 = rms_norm(tokens_f, epsilon)
        resid = tokens_f + tanh_attn * attn_out
        normed2, inverse2 = rms_norm(resid, epsilon)
        gain2 = norm2_gain * (1.0 + scale_ffn)
        ffn_in = line_gather((normed2 * gain2).astype(bf16))
        gate_up = dot(ffn_in, ffn_s)
        gate_pre, up_pre = gate_up[:, :ff_own], gate_up[:, ff_own:]
        sigmoid_g = jax.nn.sigmoid(gate_pre)
        silu_g = gate_pre * sigmoid_g
        hidden_b = (silu_g * up_pre).astype(bf16)
        d_ffn_b = (tanh_ffn * cot_all.astype(f32)).astype(bf16)
        d_hidden = dot_nt(d_ffn_b, down_s)
        silu_slope = sigmoid_g * (1.0 + gate_pre * (1.0 - sigmoid_g))
        d_gate_up = jnp.concatenate(
            [
                (d_hidden * up_pre * silu_slope).astype(bf16),
                (d_hidden * silu_g).astype(bf16),
            ],
            -1,
        )
        d_ffn_in = line_scatter(dot_nt(d_gate_up, ffn_s).astype(bf16))
        d_out = cotangent[0].astype(f32)
        grad_down = dot_tn(hidden_b, d_ffn_b).astype(bf16)
        sum_down = scatter_spread(grad_down, spread_ffn).astype(f32)
        grad_ffn = dot_tn(ffn_in, d_gate_up).astype(bf16)
        grad_ffn = grad_ffn.reshape(shards, ring, pair, rows, -1).transpose(0, 2, 1, 3, 4)
        sum_ffn = scatter_spread(grad_ffn.reshape(width, -1), spread_ffn)
        ffn_ready = sum_ffn

        sum_norm2 = jnp.sum(d_ffn_in * normed2, 0)
        d_resid = d_out + norm_back(normed2, inverse2, d_ffn_in * gain2)
        sum_gate_attn = jnp.sum(d_resid * attn_out, 0)
        d_attn_b = jnp.concatenate(ring_gather((tanh_attn * d_resid).astype(bf16)), 0)
        hidden_b, d_attn_b = tie(hidden_b, d_attn_b)
        ffn_out = line_scatter(dot(hidden_b, down_s).astype(bf16))
        mixed_out = (resid + tanh_ffn * ffn_out).astype(bf16)
        sum_gate_ffn = jnp.sum(d_out * ffn_out, 0)
        grad_out = dot_tn(mixed_b, d_attn_b).astype(bf16)
        sum_out = lax.ppermute(scatter_spread(grad_out), every, from_heads).astype(f32)
        d_mixed = dot_nt(d_attn_b, out_s).reshape(team_rows, heads, head_dim).transpose(1, 0, 2)
        grad_cross = jnp.sum(d_mixed * cross_out, axis=(1, 2)) * (1.0 - gate_own * gate_own)
        d_self_b = d_mixed.astype(bf16)
        d_cross_b = (gate_t * d_mixed).astype(bf16)

        d_cross_probs = ein("hqd,hkd->hqk", d_cross_b, values_text_b)
        d_cross_scores = (
            cross_probs
            * (d_cross_probs - jnp.sum(cross_probs * d_cross_probs, -1, keepdims=True))
        ).astype(bf16)
        d_queries = ein("hqk,hkd->hqd", d_cross_scores, keys_text_b)
        d_text_keys_n = ein("hqk,hqd->hkd", d_cross_scores, queries_b) * attn_scale
        d_text_values = ein("hqk,hqd->hkd", cross_probs_b, d_cross_b)
        if outer > 1:
            d_text_keys_n = lax.psum(d_text_keys_n, "outer")
            d_text_values = lax.psum(d_text_values, "outer")
        d_text_keys = norm_back(text_keys_n, inverse_t, d_text_keys_n)
        text_grads = jnp.stack([d_text_keys, d_text_values]).transpose(2, 0, 1, 3)
        text_grads = text_grads.reshape(cap_len, 2 * own).astype(bf16)
        if outer > 1:
            text_grads = lax.dynamic_slice_in_dim(
                text_grads, lax.axis_index("outer") * inner * cap_rows, inner * cap_rows
            )
        grad_rows = text_grads.shape[0]
        text_grads = small_gather(text_grads).reshape(inner, grad_rows, 2, own)
        text_grads = text_grads.transpose(2, 1, 0, 3).reshape(2, grad_rows, width)
        text_grads = jnp.concatenate([text_grads[0], text_grads[1]], -1)
        sum_text = scatter_spread(dot_tn(cap_own, text_grads).astype(bf16)).astype(f32)
        d_cap = dot_nt(text_grads[:, :width], key_s) + dot_nt(text_grads[:, width:], value_s)

        row_dots = jnp.sum(d_self_b.astype(f32) * self_out, -1, keepdims=True)
        soft_probs = jnp.exp(scores - log_sum)
        d_probs = ein("hqd,hkd->hqk", d_self_b, values_b)
        d_scores_b = (soft_probs * (d_probs - row_dots)).astype(bf16)
        d_queries = (d_queries + ein("hqk,hkd->hqd", d_scores_b, keys_b)) * attn_scale
        d_keys = ein("hqk,hqd->hkd", d_scores_b, queries_b) * attn_scale
        d_values = ein("hqk,hqd->hkd", soft_probs.astype(bf16), d_self_b)
        if outer > 1:
            d_keys = lax.psum_scatter(d_keys, "outer", scatter_dimension=1, tiled=True)
            d_values = lax.psum_scatter(d_values, "outer", scatter_dimension=1, tiled=True)
        d_queries_raw = norm_back(queries_n, inverse_q, rotate(d_queries, cos_tab, -sin_tab))
        d_keys_raw = norm_back(keys_n, inverse_k, rotate(d_keys, cos_tab, -sin_tab))
        d_qkv = jnp.stack([d_queries_raw, d_keys_raw, d_values]).astype(bf16)
        d_qkv = d_qkv.transpose(2, 0, 1, 3).reshape(team_rows, 3 * own)
        d_qkv, ffn_ready = tie(d_qkv, ffn_ready)
        grad_qkv = dot_tn(mix_in, d_qkv).astype(bf16)
        grad_qkv, d_mix_part = tie(grad_qkv, dot_nt(d_qkv, qkv_s).astype(bf16))
        d_mix_in = ring_scatter(row_blocks(d_mix_part))
        d_mix_in, ffn_ready = tie(d_mix_in, ffn_ready)
        sum_ffn = ffn_ready.reshape(ring, rows, 2 * ff_own)
        sum_ffn = lax.all_to_all(sum_ffn, "ring", split_axis=0, concat_axis=0, tiled=True)
        sum_gate = back_line_columns(sum_ffn[:, :, :ff_own]).astype(f32)
        sum_up = back_line_columns(sum_ffn[:, :, ff_own:]).astype(f32)
        sum_qkv = scatter_spread(grad_qkv)
        sum_qkv = swap_team(sum_qkv.reshape(inner, rows, 3 * own)).reshape(inner, rows, 3, own)
        sum_qkv = sum_qkv.transpose(1, 2, 0, 3).reshape(rows, 3 * width).astype(f32)

        sum_norm1 = jnp.sum(d_mix_in * normed1, 0)
        d_tokens = d_resid + norm_back(normed1, inverse1, d_mix_in * gain1)

        cross_slots = jnp.zeros((128,), f32)
        cross_slots = lax.dynamic_update_slice_in_dim(cross_slots, grad_cross, member * heads, 0)
        early = jnp.concatenate([sum_gate_attn, sum_norm2, sum_gate_ffn, cross_slots])
        early = small_sum(early.reshape(-1, 128))
        late = small_sum(sum_norm1.reshape(-1, 128))
        if outer > 1:
            early = lax.psum(early, "outer")
            late = lax.psum(late, "outer")
        clip_sums = jnp.concatenate([late, early], 0)
        clip_facts = jnp.concatenate([clip_sums, packed.reshape(-1, 128)], 0)
        clip_facts = lax.all_gather(clip_facts, "clip", axis=0).reshape(clips, -1)
        sums = clip_facts[:, : clip_sums.size]
        clip_facts = clip_facts[:, clip_sums.size :]
        mods = clip_facts[:, :mod_width].reshape(clips, 4, width)
        at = mod_width
        cond_all = clip_facts[:, at : at + cond_width]
        at += cond_width
        pool_all = clip_facts[:, at : at + pooled.shape[0]]
        steps_all = clip_facts[:, at + pooled.shape[0]]
        token_sums = sums[:, :mod_width].reshape(clips, 4, width)
        grad_norm1 = jnp.sum(token_sums[:, 0] * (1.0 + mods[:, 0]), 0)
        grad_norm2 = jnp.sum(token_sums[:, 2] * (1.0 + mods[:, 2]), 0)
        tanh1, tanh3 = jnp.tanh(mods[:, 1]), jnp.tanh(mods[:, 3])
        d_modulation = jnp.concatenate(
            [
                token_sums[:, 0] * norm1_gain,
                token_sums[:, 1] * (1.0 - tanh1 * tanh1),
                token_sums[:, 2] * norm2_gain,
                token_sums[:, 3] * (1.0 - tanh3 * tanh3),
            ],
            -1,
        )
        grad_bias = jnp.sum(d_modulation, 0)
        grad_cross_gate = jnp.sum(sums[:, mod_width : mod_width + head_count], 0)
        row = shard * inner + member
        cond_rows = lax.dynamic_slice_in_dim(
            jax.nn.silu(cond_all).astype(bf16).astype(f32), row * ada_rows, ada_rows, 1
        )
        sum_ada = jnp.sum(cond_rows[:, :, None] * d_modulation[:, None, :], 0)
        d_mod_clip = lax.dynamic_index_in_dim(d_modulation, lax.axis_index("clip"), 0)
        d_cond_own = dot_nt(d_mod_clip.astype(bf16), ada_s)
        d_cond_act = small_gather(d_cond_own.reshape(shards, ada_rows))
        d_cond_act = d_cond_act.transpose(1, 0, 2).reshape(1, cond_width)
        sigmoid_c = jax.nn.sigmoid(condition)
        d_condition = d_cond_act * sigmoid_c * (1.0 + condition * (1.0 - sigmoid_c))
        d_cond_all = lax.all_gather(d_condition[0], "clip", axis=0)
        d_pooled = dot_nt(d_condition.astype(bf16), pool_s).reshape(shards, -1)
        d_pooled = d_pooled[:, :pool_rows].reshape(1, -1)
        first = lax.axis_index("outer") * grad_rows
        own_mask = (first + jnp.arange(grad_rows) < lengths[0]).astype(f32)
        d_cap = (d_cap + own_mask[:, None] * d_pooled / length_f).astype(bf16)
        d_caption = back_columns(swap_team(d_cap.reshape(inner, cap_rows, -1))).astype(f32)
        embed_all = timestep_embed(steps_all, embed_width).astype(bf16).astype(f32)
        embed_rows = lax.dynamic_slice_in_dim(embed_all, row * time_rows, time_rows, 1)
        sum_time = jnp.sum(embed_rows[:, :, None] * d_cond_all[:, None, :], 0)
        pooled_rows = lax.dynamic_slice_in_dim(
            pool_all.astype(bf16).astype(f32), shard * pool_rows, pool_rows, 1
        )
        sum_pool = jnp.sum(pooled_rows[:, :, None] * d_cond_all[:, None, :], 0)
        return (
            mixed_out[None],
            d_tokens[None],
            d_caption[None],
            sum_time,
            sum_pool,
            sum_ada,
            grad_bias,
            grad_norm1,
            sum_qkv,
            sum_text[:, :width],
            sum_text[:, width:],
            grad_cross_gate,
            sum_out,
            grad_norm2,
            sum_gate,
            sum_up,
            sum_down,
        )

    return body


def solution(mesh):
    clips, members = mesh.shape["clip"], mesh.shape["seq"]

    def run(*args):
        inner = math.gcd(args[13].shape[0], members)
        outer, pair = members // inner, math.gcd(inner, 2)
        ring = inner // pair
        names = ("clip", "outer", "ring", "pair")
        fine = Mesh(mesh.devices.reshape(clips, outer, ring, pair), names)
        seq = names[1:]
        every = P(names, None)
        by_token = P("clip", seq, None)
        return jax.shard_map(
            make_body(clips, outer, ring, pair),
            mesh=fine,
            in_specs=(
                by_token,
                by_token,
                P("clip"),
                P("clip"),
                P(None, "clip", seq),
                every,
                every,
                every,
                P(),
                P(),
                every,
                every,
                every,
                P(),
                every,
                P(),
                every,
                every,
                every,
                by_token,
            ),
            out_specs=(
                by_token,
                by_token,
                by_token,
                every,
                every,
                every,
                P(),
                P(),
                every,
                every,
                every,
                P(),
                every,
                P(),
                every,
                every,
                every,
            ),
            check_vma=False,
        )(*args)

    return run
```

```python
import math

import jax
import jax.numpy as jnp
from jax import lax
from jax.sharding import Mesh
from jax.sharding import PartitionSpec as P

epsilon = 1e-05
head_eps = 1e-06
big_negative = -1e30
f32 = jnp.float32
bf16 = jnp.bfloat16


def rope_tables(posint, half_dim):
    pair_ids = jnp.arange(half_dim)
    first_cut = half_dim // 4
    second_cut = first_cut + (half_dim - first_cut) // 2
    group_of = (pair_ids >= first_cut).astype(jnp.int32) + (pair_ids >= second_cut).astype(
        jnp.int32
    )
    starts = jnp.where(group_of == 0, 0, jnp.where(group_of == 1, first_cut, second_cut))
    counts = jnp.where(
        group_of == 0,
        first_cut,
        jnp.where(group_of == 1, second_cut - first_cut, half_dim - second_cut),
    )
    frequency = jnp.exp(
        -math.log(10000.0) * (pair_ids - starts).astype(f32) / counts.astype(f32)
    )
    spots = posint.astype(f32)[:, :, None]
    coords = jnp.where(group_of == 0, spots[0], jnp.where(group_of == 1, spots[1], spots[2]))
    angles = coords * frequency[None, :]
    return (jnp.cos(angles), jnp.sin(angles))


def rotate(vector, cos_tab, sin_tab):
    half_dim = cos_tab.shape[-1]
    front = vector[..., :half_dim]
    behind = vector[..., half_dim:]
    return jnp.concatenate(
        [front * cos_tab - behind * sin_tab, front * sin_tab + behind * cos_tab], -1
    )


def rms_norm(vector, eps_value):
    inverse = lax.rsqrt(jnp.mean(vector * vector, -1, keepdims=True) + eps_value)
    return (vector * inverse, inverse)


def norm_back(normed, inverse, gradient):
    return inverse * (gradient - normed * jnp.mean(gradient * normed, -1, keepdims=True))


def timestep_embed(time_step, embed_width):
    half_dim = embed_width // 2
    frequency = jnp.exp(-math.log(10000.0) * jnp.arange(half_dim, dtype=f32) / half_dim)
    angles = time_step.astype(f32)[..., None] * frequency
    return jnp.concatenate([jnp.cos(angles), jnp.sin(angles)], -1)


def dot(a, b):
    return jnp.dot(a, b, preferred_element_type=f32)


def dot_tn(a, b):
    return lax.dot_general(a, b, (((0,), (0,)), ((), ())), preferred_element_type=f32)


def dot_nt(a, b):
    return lax.dot_general(a, b, (((1,), (1,)), ((), ())), preferred_element_type=f32)


def ein(spec, a, b):
    return jnp.einsum(spec, a, b, preferred_element_type=f32)


def tie(*arrays):
    return lax.optimization_barrier(arrays)


def make_body(clips, outer, ring, pair):
    inner = ring * pair
    shards = clips * outer
    team = ("ring", "pair")
    spread = ("clip", "outer") if outer > 1 else "clip"
    spread_ffn = ("clip", "outer", "pair")
    every = ("clip", "outer", "ring", "pair")
    forward = [(z, (z + 1) % ring) for z in range(ring)]
    crossed = [(x, (x + 1) % pair) for x in range(pair)]
    slots = [(k, e) for k in range(ring) for e in range(pair)]

    def swap_team(x):
        return lax.all_to_all(x, team, split_axis=0, concat_axis=0, tiled=True)

    def gather_spread(x, axes=spread):
        return lax.all_gather(x, axes, axis=0, tiled=True)

    def scatter_spread(x, axes=spread):
        return lax.psum_scatter(x, axes, scatter_dimension=0, tiled=True)

    def ring_gather(x):
        parts, now = [], x
        for k in range(ring):
            parts.append(now)
            other = now
            for _ in range(1, pair):
                other = lax.ppermute(other, "pair", crossed)
                parts.append(other)
            if k + 1 < ring:
                now = lax.ppermute(now, "ring", forward)
        return parts

    def ring_scatter(block_of):
        passed = None
        for step in range(1, ring + 1):
            k = step % ring
            total = block_of(k, 0).astype(f32)
            if pair > 1:
                total = total + lax.ppermute(block_of(k, 1), "pair", crossed).astype(f32)
            if passed is not None:
                total = total + passed.astype(f32)
            if step < ring:
                passed = lax.ppermute(total.astype(bf16), "ring", forward)
        return total

    def row_blocks(x):
        rows = x.shape[0] // inner
        return lambda k, e: x[(k * pair + e) * rows : (k * pair + e + 1) * rows]

    def line_gather(x):
        parts = [x]
        for _ in range(1, ring):
            parts.append(lax.ppermute(parts[-1], "ring", forward))
        return jnp.concatenate(parts, 0)

    def line_scatter(x):
        rows = x.shape[0] // ring
        passed = None
        for step in range(1, ring + 1):
            k = step % ring
            total = x[k * rows : (k + 1) * rows].astype(f32)
            if passed is not None:
                total = total + passed.astype(f32)
            if step < ring:
                passed = lax.ppermute(total.astype(bf16), "ring", forward)
        return total

    def small_sum(x):
        for axis, size in (("pair", pair), ("ring", ring)):
            if size & (size - 1):
                x = lax.psum(x, axis)
                continue
            hop = 1
            while hop < size:
                x = x + lax.ppermute(x, axis, [(i, i ^ hop) for i in range(size)])
                hop *= 2
        return x

    def small_gather(x):
        return swap_team(jnp.broadcast_to(x, (inner,) + x.shape))

    def in_order(parts):
        z, y = lax.axis_index("ring"), lax.axis_index("pair")
        if pair > 1:
            front = [jnp.where(y == 0, parts[2 * k], parts[2 * k + 1]) for k in range(ring)]
            behind = [jnp.where(y == 0, parts[2 * k + 1], parts[2 * k]) for k in range(ring)]
            rows = [jnp.stack([f, g]) for f, g in zip(front, behind)]
        else:
            rows = [part[None] for part in parts]
        twice = jnp.stack((rows[1:] + rows)[::-1])
        whole = lax.dynamic_slice_in_dim(twice, ring - 1 - z, ring)
        return whole.reshape((inner,) + parts[0].shape)

    def slot_blocks(x):
        z, y = lax.axis_index("ring"), lax.axis_index("pair")

        def block_of(k, e):
            spot = lax.rem(z + ring - k, ring) * pair + lax.rem(y + pair - e, pair)
            return lax.dynamic_index_in_dim(x, spot, 0, keepdims=False)

        return block_of

    def by_columns(w):
        rows, columns = w.shape
        blocks = w.reshape(rows, shards, inner, columns // (shards * inner))
        return blocks.transpose(2, 0, 1, 3).reshape(inner, rows, columns // inner)

    def back_columns(w):
        _, rows, columns = w.shape
        blocks = w.reshape(inner, rows, shards, columns // shards)
        return blocks.transpose(1, 2, 0, 3).reshape(rows, inner * columns)

    def line_columns(w):
        rows, columns = w.shape
        blocks = w.reshape(rows, shards, ring, columns // (shards * ring))
        return blocks.transpose(2, 0, 1, 3).reshape(ring, rows, columns // ring)

    def back_line_columns(w):
        _, rows, columns = w.shape
        blocks = w.reshape(ring, rows, shards, columns // shards)
        return blocks.transpose(1, 2, 0, 3).reshape(rows, ring * columns)

    def body(
        tokens,
        caption,
        lengths,
        timesteps,
        positions,
        w_time,
        w_pool,
        w_ada,
        b_ada,
        norm1_gain,
        w_qkv,
        w_key_text,
        w_value_text,
        cross_gate,
        w_out,
        norm2_gain,
        w_gate,
        w_up,
        w_down,
        cotangent,
    ):
        head_count = cross_gate.shape[0]
        width = tokens.shape[2]
        head_dim = width // head_count
        heads = head_count // inner
        own = heads * head_dim
        tok_rows = tokens.shape[1]
        team_rows = tok_rows * inner
        cap_rows = caption.shape[1]
        cond_width = w_pool.shape[1]
        mod_width = b_ada.shape[0]
        attn_scale = 1.0 / math.sqrt(head_dim)
        member = lax.axis_index(team)
        shard = lax.axis_index(spread)
        length_f = lengths[0].astype(f32)

        cap_blocks = by_columns(caption[0])
        cap_part = swap_team(cap_blocks).reshape(inner * cap_rows, -1)
        cap_own = cap_part
        if outer > 1:
            cap_part = lax.all_gather(cap_part, "outer", axis=0, tiled=True)
        cap_len = cap_part.shape[0]
        pool_rows, time_rows, ada_rows = w_pool.shape[0], w_time.shape[0], w_ada.shape[0]
        pool_s = gather_spread(jnp.concatenate([w_pool, w_time], 0))
        ada_s = gather_spread(w_ada)
        rows = w_qkv.shape[0]
        qkv_blocks = w_qkv.reshape(rows, 3, inner, own).transpose(2, 0, 1, 3)
        qkv_blocks = qkv_blocks.reshape(inner, rows, 3 * own)
        qkv_s = gather_spread(swap_team(qkv_blocks).reshape(inner * rows, 3 * own))
        spots = positions[:, 0, :].astype(bf16).T
        spots = jnp.concatenate([spots, jnp.zeros((tok_rows, 125), bf16)], -1)
        tokens_all = jnp.concatenate(
            ring_gather(jnp.concatenate([tokens[0], spots], -1)), 0
        )
        spots = tokens_all[:, width : width + 3].astype(f32).T
        tokens_all = tokens_all[:, :width]
        to_heads = [
            (r, (r % shards) * inner + r // shards) for r in range(shards * inner)
        ]
        from_heads = [(b, a) for a, b in to_heads]
        out_rows = lax.ppermute(w_out, every, to_heads)
        text_rows = w_key_text.shape[0]

        cap_mask = (jnp.arange(cap_len) < lengths[0]).astype(f32)
        pooled = jnp.sum(cap_part.astype(f32) * cap_mask[:, None], 0) / length_f
        pooled_b = pooled.astype(bf16)
        embed_width = time_rows * shards * inner
        time_embed = timestep_embed(timesteps[0], embed_width).astype(bf16)
        time_own = lax.dynamic_index_in_dim(
            time_embed.reshape(shards, inner, time_rows), member, 1, keepdims=False
        )
        facts = jnp.concatenate([pooled_b.reshape(shards, pool_rows), time_own], 1)
        condition = small_sum(dot(facts.reshape(1, -1), pool_s))
        cond_b = jax.nn.silu(condition).astype(bf16)
        cond_own = lax.dynamic_index_in_dim(
            cond_b.reshape(shards, inner, ada_rows), member, 1, keepdims=False
        ).reshape(1, -1)
        modulation = small_sum(dot(cond_own, ada_s)).reshape(-1) + b_ada
        scale_attn, gate_attn, scale_ffn, gate_ffn = jnp.split(modulation, 4)
        tanh_attn = jnp.tanh(gate_attn)
        tanh_ffn = jnp.tanh(gate_ffn)
        text_pack = jnp.concatenate([w_key_text, w_value_text, out_rows], 0)
        text_pack = gather_spread(text_pack).reshape(shards, -1, width)
        key_s = text_pack[:, :text_rows].reshape(-1, width)
        value_s = text_pack[:, text_rows : 2 * text_rows].reshape(-1, width)
        out_s = text_pack[:, 2 * text_rows :].reshape(-1, width)
        gate_in, up_in, down_in, condition = tie(w_gate, w_up, w_down, condition)
        ffn_blocks = jnp.concatenate([line_columns(gate_in), line_columns(up_in)], -1)
        ffn_blocks = lax.all_to_all(ffn_blocks, "ring", split_axis=0, concat_axis=0, tiled=True)
        ffn_s = gather_spread(ffn_blocks.reshape(ring * rows, -1), spread_ffn)
        ffn_s = ffn_s.reshape(shards, pair, ring, rows, -1).transpose(0, 2, 1, 3, 4)
        ffn_s = ffn_s.reshape(width, -1)
        down_s = gather_spread(down_in, spread_ffn)
        ff_own = down_s.shape[0]
        packed = jnp.concatenate(
            [
                modulation,
                condition[0],
                pooled,
                jnp.full((128,), timesteps[0].astype(f32)),
            ]
        )

        normed_all, _ = rms_norm(tokens_all.astype(f32), epsilon)
        gain1 = norm1_gain * (1.0 + scale_attn)
        mix_in = (normed_all * gain1).astype(bf16)
        cot_in, mix_in = tie(cotangent[0], mix_in)
        cot_all = line_gather(cot_in)
        qkv_own = dot(mix_in, qkv_s).reshape(team_rows, 3, heads, head_dim).transpose(1, 2, 0, 3)
        cos_tab, sin_tab = rope_tables(spots, head_dim // 2)
        queries_n, inverse_q = rms_norm(qkv_own[0], head_eps)
        keys_n, inverse_k = rms_norm(qkv_own[1], head_eps)
        queries_b = rotate(queries_n, cos_tab, sin_tab).astype(bf16)
        keys_b = rotate(keys_n, cos_tab, sin_tab).astype(bf16)
        values_b = qkv_own[2].astype(bf16)
        if outer > 1:
            keys_b = lax.all_gather(keys_b, "outer", axis=1, tiled=True)
            values_b = lax.all_gather(values_b, "outer", axis=1, tiled=True)
        scores = ein("hqd,hkd->hqk", queries_b, keys_b) * attn_scale
        top = jnp.max(scores, -1, keepdims=True)
        raised = jnp.exp(scores - top)
        total = jnp.sum(raised, -1, keepdims=True)
        self_out = ein("hqk,hkd->hqd", raised.astype(bf16), values_b) / total
        log_sum = top + jnp.log(total)

        text_part = jnp.stack([dot(cap_part, key_s), dot(cap_part, value_s)]).astype(bf16)
        text_part = text_part.reshape(2, cap_len, inner, own).transpose(2, 1, 0, 3)
        text_own = swap_team(text_part.reshape(inner, cap_len, 2 * own))
        text_own = jnp.sum(text_own.astype(f32), 0)
        text_own = text_own.reshape(cap_len, 2, heads, head_dim).transpose(1, 2, 0, 3)
        text_keys_n, inverse_t = rms_norm(text_own[0], head_eps)
        keys_text_b = text_keys_n.astype(bf16)
        values_text_b = text_own[1].astype(bf16)
        cross_scores = ein("hqd,hkd->hqk", queries_b, keys_text_b) * attn_scale
        cross_scores = jnp.where(cap_mask > 0, cross_scores, big_negative)
        cross_probs = jax.nn.softmax(cross_scores, axis=-1)
        cross_probs_b = cross_probs.astype(bf16)
        cross_out = ein("hqk,hkd->hqd", cross_probs_b, values_text_b)
        gate_own = jnp.tanh(lax.dynamic_slice_in_dim(cross_gate, member * heads, heads))
        gate_t = gate_own[:, None, None]
        mixed = self_out + gate_t * cross_out
        mixed_b = mixed.transpose(1, 0, 2).reshape(team_rows, own).astype(bf16)
        attn_out = ring_scatter(row_blocks(dot(mixed_b, out_s).astype(bf16)))

        tokens_f = tokens[0].astype(f32)
        normed1, inverse1 = rms_norm(tokens_f, epsilon)
        resid = tokens_f + tanh_attn * attn_out
        normed2, inverse2 = rms_norm(resid, epsilon)
        gain2 = norm2_gain * (1.0 + scale_ffn)
        ffn_in = line_gather((normed2 * gain2).astype(bf16))
        gate_up = dot(ffn_in, ffn_s)
        gate_pre, up_pre = gate_up[:, :ff_own], gate_up[:, ff_own:]
        sigmoid_g = jax.nn.sigmoid(gate_pre)
        silu_g = gate_pre * sigmoid_g
        hidden_b = (silu_g * up_pre).astype(bf16)
        d_ffn_b = (tanh_ffn * cot_all.astype(f32)).astype(bf16)
        d_hidden = dot_nt(d_ffn_b, down_s)
        silu_slope = sigmoid_g * (1.0 + gate_pre * (1.0 - sigmoid_g))
        d_gate_up = jnp.concatenate(
            [
                (d_hidden * up_pre * silu_slope).astype(bf16),
                (d_hidden * silu_g).astype(bf16),
            ],
            -1,
        )
        d_ffn_part = dot_nt(d_gate_up, ffn_s).astype(bf16)
        d_ffn_part, d_gate_up = tie(d_ffn_part, d_gate_up)
        d_ffn_in = line_scatter(d_ffn_part)
        d_out = cotangent[0].astype(f32)
        grad_down = dot_tn(hidden_b, d_ffn_b).astype(bf16)
        sum_down = scatter_spread(grad_down, spread_ffn).astype(f32)
        grad_ffn = dot_tn(ffn_in, d_gate_up).astype(bf16)
        grad_ffn = grad_ffn.reshape(shards, ring, pair, rows, -1).transpose(0, 2, 1, 3, 4)
        sum_ffn = scatter_spread(grad_ffn.reshape(width, -1), spread_ffn)
        ffn_ready = sum_ffn

        sum_norm2 = jnp.sum(d_ffn_in * normed2, 0)
        d_resid = d_out + norm_back(normed2, inverse2, d_ffn_in * gain2)
        sum_gate_attn = jnp.sum(d_resid * attn_out, 0)
        d_attn_b = jnp.concatenate(ring_gather((tanh_attn * d_resid).astype(bf16)), 0)
        hidden_b, d_attn_b = tie(hidden_b, d_attn_b)
        ffn_out = line_scatter(dot(hidden_b, down_s).astype(bf16))
        mixed_out = (resid + tanh_ffn * ffn_out).astype(bf16)
        sum_gate_ffn = jnp.sum(d_out * ffn_out, 0)
        grad_out = dot_tn(mixed_b, d_attn_b).astype(bf16)
        sum_out = lax.ppermute(scatter_spread(grad_out), every, from_heads).astype(f32)
        d_mixed = dot_nt(d_attn_b, out_s).reshape(team_rows, heads, head_dim).transpose(1, 0, 2)
        grad_cross = jnp.sum(d_mixed * cross_out, axis=(1, 2)) * (1.0 - gate_own * gate_own)
        d_self_b = d_mixed.astype(bf16)
        d_cross_b = (gate_t * d_mixed).astype(bf16)

        d_cross_probs = ein("hqd,hkd->hqk", d_cross_b, values_text_b)
        d_cross_scores = (
            cross_probs
            * (d_cross_probs - jnp.sum(cross_probs * d_cross_probs, -1, keepdims=True))
        ).astype(bf16)
        d_queries = ein("hqk,hkd->hqd", d_cross_scores, keys_text_b)
        d_text_keys_n = ein("hqk,hqd->hkd", d_cross_scores, queries_b) * attn_scale
        d_text_values = ein("hqk,hqd->hkd", cross_probs_b, d_cross_b)
        if outer > 1:
            d_text_keys_n = lax.psum(d_text_keys_n, "outer")
            d_text_values = lax.psum(d_text_values, "outer")
        d_text_keys = norm_back(text_keys_n, inverse_t, d_text_keys_n)
        text_grads = jnp.stack([d_text_keys, d_text_values]).transpose(2, 0, 1, 3)
        text_grads = text_grads.reshape(cap_len, 2 * own).astype(bf16)
        if outer > 1:
            text_grads = lax.dynamic_slice_in_dim(
                text_grads, lax.axis_index("outer") * inner * cap_rows, inner * cap_rows
            )
        grad_rows = text_grads.shape[0]
        text_grads = small_gather(text_grads).reshape(inner, grad_rows, 2, own)
        text_grads = text_grads.transpose(2, 1, 0, 3).reshape(2, grad_rows, width)
        text_grads = jnp.concatenate([text_grads[0], text_grads[1]], -1)
        sum_text = scatter_spread(dot_tn(cap_own, text_grads).astype(bf16)).astype(f32)
        d_cap = dot_nt(text_grads[:, :width], key_s) + dot_nt(text_grads[:, width:], value_s)

        row_dots = jnp.sum(d_self_b.astype(f32) * self_out, -1, keepdims=True)
        soft_probs = jnp.exp(scores - log_sum)
        d_probs = ein("hqd,hkd->hqk", d_self_b, values_b)
        d_scores_b = (soft_probs * (d_probs - row_dots)).astype(bf16)
        d_queries = (d_queries + ein("hqk,hkd->hqd", d_scores_b, keys_b)) * attn_scale
        d_keys = ein("hqk,hqd->hkd", d_scores_b, queries_b) * attn_scale
        d_values = ein("hqk,hqd->hkd", soft_probs.astype(bf16), d_self_b)
        if outer > 1:
            d_keys = lax.psum_scatter(d_keys, "outer", scatter_dimension=1, tiled=True)
            d_values = lax.psum_scatter(d_values, "outer", scatter_dimension=1, tiled=True)
        d_queries_raw = norm_back(queries_n, inverse_q, rotate(d_queries, cos_tab, -sin_tab))
        d_keys_raw = norm_back(keys_n, inverse_k, rotate(d_keys, cos_tab, -sin_tab))
        d_qkv = jnp.stack([d_queries_raw, d_keys_raw, d_values]).astype(bf16)
        d_qkv = d_qkv.transpose(2, 0, 1, 3).reshape(team_rows, 3 * own)
        d_qkv, ffn_ready = tie(d_qkv, ffn_ready)
        grad_qkv = dot_tn(mix_in, d_qkv).astype(bf16)
        grad_qkv, d_mix_part = tie(grad_qkv, dot_nt(d_qkv, qkv_s).astype(bf16))
        d_mix_in = ring_scatter(row_blocks(d_mix_part))
        d_mix_in, ffn_ready = tie(d_mix_in, ffn_ready)
        sum_ffn = ffn_ready.reshape(ring, rows, 2 * ff_own)
        sum_ffn = lax.all_to_all(sum_ffn, "ring", split_axis=0, concat_axis=0, tiled=True)
        sum_gate = back_line_columns(sum_ffn[:, :, :ff_own]).astype(f32)
        sum_up = back_line_columns(sum_ffn[:, :, ff_own:]).astype(f32)
        sum_qkv = scatter_spread(grad_qkv)
        sum_qkv = swap_team(sum_qkv.reshape(inner, rows, 3 * own)).reshape(inner, rows, 3, own)
        sum_qkv = sum_qkv.transpose(1, 2, 0, 3).reshape(rows, 3 * width).astype(f32)

        sum_norm1 = jnp.sum(d_mix_in * normed1, 0)
        d_tokens = d_resid + norm_back(normed1, inverse1, d_mix_in * gain1)

        cross_slots = jnp.zeros((128,), f32)
        cross_slots = lax.dynamic_update_slice_in_dim(cross_slots, grad_cross, member * heads, 0)
        early = jnp.concatenate([sum_gate_attn, sum_norm2, sum_gate_ffn, cross_slots])
        early = small_sum(early.reshape(-1, 128))
        late = small_sum(sum_norm1.reshape(-1, 128))
        if outer > 1:
            early = lax.psum(early, "outer")
            late = lax.psum(late, "outer")
        clip_sums = jnp.concatenate([late, early], 0)
        clip_facts = jnp.concatenate([clip_sums, packed.reshape(-1, 128)], 0)
        clip_facts = lax.all_gather(clip_facts, "clip", axis=0).reshape(clips, -1)
        sums = clip_facts[:, : clip_sums.size]
        clip_facts = clip_facts[:, clip_sums.size :]
        mods = clip_facts[:, :mod_width].reshape(clips, 4, width)
        at = mod_width
        cond_all = clip_facts[:, at : at + cond_width]
        at += cond_width
        pool_all = clip_facts[:, at : at + pooled.shape[0]]
        steps_all = clip_facts[:, at + pooled.shape[0]]
        token_sums = sums[:, :mod_width].reshape(clips, 4, width)
        grad_norm1 = jnp.sum(token_sums[:, 0] * (1.0 + mods[:, 0]), 0)
        grad_norm2 = jnp.sum(token_sums[:, 2] * (1.0 + mods[:, 2]), 0)
        tanh1, tanh3 = jnp.tanh(mods[:, 1]), jnp.tanh(mods[:, 3])
        d_modulation = jnp.concatenate(
            [
                token_sums[:, 0] * norm1_gain,
                token_sums[:, 1] * (1.0 - tanh1 * tanh1),
                token_sums[:, 2] * norm2_gain,
                token_sums[:, 3] * (1.0 - tanh3 * tanh3),
            ],
            -1,
        )
        grad_bias = jnp.sum(d_modulation, 0)
        grad_cross_gate = jnp.sum(sums[:, mod_width : mod_width + head_count], 0)
        row = shard * inner + member
        cond_rows = lax.dynamic_slice_in_dim(
            jax.nn.silu(cond_all).astype(bf16).astype(f32), row * ada_rows, ada_rows, 1
        )
        sum_ada = jnp.sum(cond_rows[:, :, None] * d_modulation[:, None, :], 0)
        d_mod_clip = lax.dynamic_index_in_dim(d_modulation, lax.axis_index("clip"), 0)
        d_cond_own = dot_nt(d_mod_clip.astype(bf16), ada_s)
        d_cond_act = small_gather(d_cond_own.reshape(shards, ada_rows))
        d_cond_act = d_cond_act.transpose(1, 0, 2).reshape(1, cond_width)
        sigmoid_c = jax.nn.sigmoid(condition)
        d_condition = d_cond_act * sigmoid_c * (1.0 + condition * (1.0 - sigmoid_c))
        d_cond_all = lax.all_gather(d_condition[0], "clip", axis=0)
        d_pooled = dot_nt(d_condition.astype(bf16), pool_s).reshape(shards, -1)
        d_pooled = d_pooled[:, :pool_rows].reshape(1, -1)
        first = lax.axis_index("outer") * grad_rows
        own_mask = (first + jnp.arange(grad_rows) < lengths[0]).astype(f32)
        d_cap = (d_cap + own_mask[:, None] * d_pooled / length_f).astype(bf16)
        d_caption = back_columns(swap_team(d_cap.reshape(inner, cap_rows, -1))).astype(f32)
        embed_all = timestep_embed(steps_all, embed_width).astype(bf16).astype(f32)
        embed_rows = lax.dynamic_slice_in_dim(embed_all, row * time_rows, time_rows, 1)
        sum_time = jnp.sum(embed_rows[:, :, None] * d_cond_all[:, None, :], 0)
        pooled_rows = lax.dynamic_slice_in_dim(
            pool_all.astype(bf16).astype(f32), shard * pool_rows, pool_rows, 1
        )
        sum_pool = jnp.sum(pooled_rows[:, :, None] * d_cond_all[:, None, :], 0)
        return (
            mixed_out[None],
            d_tokens[None],
            d_caption[None],
            sum_time,
            sum_pool,
            sum_ada,
            grad_bias,
            grad_norm1,
            sum_qkv,
            sum_text[:, :width],
            sum_text[:, width:],
            grad_cross_gate,
            sum_out,
            grad_norm2,
            sum_gate,
            sum_up,
            sum_down,
        )

    return body


def solution(mesh):
    clips, members = mesh.shape["clip"], mesh.shape["seq"]

    def run(*args):
        inner = math.gcd(args[13].shape[0], members)
        outer, pair = members // inner, math.gcd(inner, 2)
        ring = inner // pair
        names = ("clip", "outer", "ring", "pair")
        fine = Mesh(mesh.devices.reshape(clips, outer, ring, pair), names)
        seq = names[1:]
        every = P(names, None)
        by_token = P("clip", seq, None)
        return jax.shard_map(
            make_body(clips, outer, ring, pair),
            mesh=fine,
            in_specs=(
                by_token,
                by_token,
                P("clip"),
                P("clip"),
                P(None, "clip", seq),
                every,
                every,
                every,
                P(),
                P(),
                every,
                every,
                every,
                P(),
                every,
                P(),
                every,
                every,
                every,
                by_token,
            ),
            out_specs=(
                by_token,
                by_token,
                by_token,
                every,
                every,
                every,
                P(),
                P(),
                every,
                every,
                every,
                P(),
                every,
                P(),
                every,
                every,
                every,
            ),
            check_vma=False,
        )(*args)

    return run
```
